32 devices in a mesh: row: 4 (over y, x), col: 8 (over z, core).
Axes of the slice: x: 2, y: 2, z: 4, core: 2. Of those that a mesh axis runs over, the one named last changes fastest.
Arguments:
- pair: bfloat16 [320, 320, 128], P('row', 'col'), may hold values from -6 to 6
- block_chain: int32 [5], replicated, may hold values from 0 to 1, never falling along the last dimension, each value on 1 to 4 neighbouring positions
- block_valid: int32 [5], replicated, may hold values 0 or 1
- tri_norm_gain: float32 [128], replicated, may hold values from 0.25 to 1.75
- tri_norm_bias: float32 [128], replicated, may hold values from -3 to 3
- tri_in_weight: bfloat16 [128, 512], replicated, may hold values from -0.5 to 0.5
- tri_gate_weight: bfloat16 [128, 128], replicated, may hold values from -0.5 to 0.5
- out_norm_gain: float32 [128], replicated, may hold values from 0.25 to 1.75
- out_norm_bias: float32 [128], replicated, may hold values from -3 to 3
- tri_out_weight: bfloat16 [128, 128], replicated, may hold values from -0.5 to 0.5
- att_norm_gain: float32 [128], replicated, may hold values from 0.25 to 1.75
- att_norm_bias: float32 [128], replicated, may hold values from -3 to 3
- qkvg_weight: bfloat16 [128, 512], replicated, may hold values from -0.5 to 0.5
- bias_weight: bfloat16 [128, 4], replicated, may hold values from -1 to 1
- inter_chain: float32 [4], replicated, may hold values from -3 to 3
- att_out_weight: bfloat16 [128, 128], replicated, may hold values from -0.5 to 0.5
Outputs:
- pair_out: bfloat16 [320, 320, 128], P('row', 'col')
The draws below stay inside these ranges and needn't reach their ends.
Inputs may be any that keep to these rules, and one draw needn't show every extreme that they name: `block_chain`: chain numbers never fall along the crop; each chain covers 1 to 4 blocks and every number from 0 up appears.
All inputs are finite; a program needn't handle non-finite values.
Results may differ from the reference program's by a relative error of at most 0.0095.
Values may be sent and summed in bfloat16 or wider, within the bound.
A program may use at most 128 MiB of HBM per device.

```python
import math
import jax
import jax.numpy as jnp
import numpy as np
from jax import lax

C = 128
CH = 128
H = 4
DH = 32
MB = 64
N = 320
NBLK = 5
HD = 128


def with_ends(values, own_key, least, high):
    longest = values.shape.index(max(values.shape))
    spots = []
    for shift in (0, 1):
        where = [jax.random.randint(jax.random.fold_in(own_key, axis), (), 0, length) for axis, length in enumerate(values.shape)]
        where[longest] = (where[longest] + shift) % values.shape[longest]
        spots.append(tuple(where))
    return values.at[spots[0]].set(least).at[spots[1]].set(high)


def block_scale(rng, extent, pieces, smallest, top_value):
    factor_of = 1.0
    for axis_at, blocks in pieces:
        heights = jax.random.uniform(jax.random.fold_in(jax.random.fold_in(rng, 6), axis_at), (blocks,), jnp.float32, smallest / len(pieces), top_value / len(pieces))
        factor_of = factor_of * jnp.repeat(jnp.exp(heights), extent[axis_at] // blocks).reshape((-1,) + (1,) * (len(extent) - 1 - axis_at))
    return factor_of


def length_profile(number_of, total, most, skew):
    weights = [(1 << 20) // math.isqrt(grade ** skew) + 1 for grade in range(2, number_of + 1)]
    spare, given = total - most - (number_of - 1), [1] * (number_of - 1)
    while spare > 0:
        free = [i for i in range(number_of - 1) if given[i] < most]
        pool, left = sum([weights[i] for i in free]), spare
        for i in free:
            more = min(most - given[i], max(1, left * weights[i] // pool), spare)
            given[i] = given[i] + more
            spare = spare - more
    return np.array([most] + given)


def ragged(rng, amount, total, bound, skew):
    if amount == 2:
        one = jax.random.randint(rng, (), max(1, total - bound), min(bound, total - 1) + 1)
        return jnp.stack([one, total - one])
    sizes = jnp.asarray(length_profile(amount, total, bound, skew), jnp.int32)
    twos = (amount - 1) // 2
    donor, sink = sizes[1:1 + 2 * twos:2], sizes[2:2 + 2 * twos:2]
    room = jnp.minimum(donor - 1, bound - sink)
    moved = jax.random.randint(jax.random.fold_in(rng, 1), (twos,), 0, 1 << 20) % (room + 1)
    sizes = sizes.at[1:1 + 2 * twos:2].set(donor - moved).at[2:2 + 2 * twos:2].set(sink + moved)
    return sizes[jax.random.permutation(jax.random.fold_in(rng, 2), amount)]


def bell_draw(stream_key, extent, width, most, shards=(), kind=jnp.bfloat16):
    entries = jax.random.normal(stream_key, extent, jnp.float32) * width
    if len(shards) > 0:
        entries = block_scale(stream_key, extent, shards, -0.22, 0.18) * entries
    return jnp.clip(entries, min=-most, max=most).astype(kind)


def setup_inputs(seed: int = 0) -> dict:
    arg_keys = jax.random.split(jax.random.key(seed), 17)
    pair = bell_draw(arg_keys[0], (N, N, C), 1.0, 6.0, ((0, 4), (1, 8)))
    block_chain = jnp.searchsorted(jnp.cumsum(ragged(arg_keys[1], NBLK // 2, NBLK, 4, 0)), jnp.arange(NBLK), side="right").astype(jnp.int32)
    block_valid = with_ends((jax.random.randint(arg_keys[2], (NBLK,), 0, 4) < 3).astype(jnp.int32), jax.random.fold_in(arg_keys[2], 1), 0, 1)
    tri_norm_gain = jnp.clip(1.0 + 0.15 * jax.random.normal(arg_keys[3], (C,), jnp.float32), 0.25, 1.75)
    tri_norm_bias = bell_draw(arg_keys[4], (C,), 0.5, 3.0, (), jnp.float32)
    tri_in_weight = bell_draw(arg_keys[5], (C, 4 * CH), C ** -0.5, 0.5)
    tri_gate_weight = bell_draw(arg_keys[6], (C, C), C ** -0.5, 0.5)
    out_norm_gain = jnp.clip(1.0 + 0.15 * jax.random.normal(arg_keys[7], (CH,), jnp.float32), 0.25, 1.75)
    out_norm_bias = bell_draw(arg_keys[8], (CH,), 0.5, 3.0, (), jnp.float32)
    tri_out_weight = bell_draw(arg_keys[9], (CH, C), CH ** -0.5, 0.5)
    att_norm_gain = jnp.clip(1.0 + 0.15 * jax.random.normal(arg_keys[10], (C,), jnp.float32), 0.25, 1.75)
    att_norm_bias = bell_draw(arg_keys[11], (C,), 0.5, 3.0, (), jnp.float32)
    qkvg_weight = bell_draw(arg_keys[12], (C, 4 * HD), C ** -0.5, 0.5)
    bias_weight = bell_draw(arg_keys[13], (C, H), (C // 4) ** -0.5, 1.0)
    inter_chain = jnp.clip(jax.random.uniform(arg_keys[14], (H,), jnp.float32, -3.0, 3.0), -3.0, 3.0)
    att_out_weight = bell_draw(arg_keys[15], (HD, C), HD ** -0.5, 0.5)
    return {"pair": pair, "block_chain": block_chain, "block_valid": block_valid, "tri_norm_gain": tri_norm_gain, "tri_norm_bias": tri_norm_bias, "tri_in_weight": tri_in_weight, "tri_gate_weight": tri_gate_weight, "out_norm_gain": out_norm_gain, "out_norm_bias": out_norm_bias, "tri_out_weight": tri_out_weight, "att_norm_gain": att_norm_gain, "att_norm_bias": att_norm_bias, "qkvg_weight": qkvg_weight, "bias_weight": bias_weight, "inter_chain": inter_chain, "att_out_weight": att_out_weight}


MASK_NEG = 10000.0
EPS = 1e-05

def layer_norm(values, gain, shift):
    middle = lax.optimization_barrier(jnp.mean(values, axis=-1, keepdims=True))
    centred = values - middle
    spread = lax.optimization_barrier(jnp.mean(centred * centred, axis=-1, keepdims=True))
    return centred * lax.rsqrt(spread + EPS) * gain + shift

def extra_terms(bias_part, inter_chain, key_chain, query_chain, key_valid):
    crossing = (key_chain[:, None] != query_chain[None, :]).astype(jnp.float32)
    masking = MASK_NEG * (key_valid - 1.0)
    return bias_part.astype(jnp.float32) + inter_chain[:, None, None] * crossing[None] + masking[None, :, None]

def attend(queries, keys, values, extra):
    scores = jnp.einsum('khd,ihd->hki', keys.astype(jnp.float32), queries.astype(jnp.float32)) + extra
    highest = lax.optimization_barrier(jnp.max(scores, axis=1, keepdims=True))
    powers = jnp.exp(scores - highest)
    weights = (powers / lax.optimization_barrier(jnp.sum(powers, axis=1, keepdims=True))).astype(jnp.bfloat16)
    return jnp.einsum('hki,khd->ihd', weights.astype(jnp.float32), values.astype(jnp.float32))

def reference(pair, block_chain, block_valid, tri_norm_gain, tri_norm_bias, tri_in_weight, tri_gate_weight, out_norm_gain, out_norm_bias, tri_out_weight, att_norm_gain, att_norm_bias, qkvg_weight, bias_weight, inter_chain, att_out_weight):
    residue_valid = jnp.repeat(block_valid, MB).astype(jnp.float32)
    residue_chain = jnp.repeat(block_chain, MB)
    pair_mask = (residue_valid[:, None] * residue_valid[None, :])[:, :, None]
    tri_normed = layer_norm(pair.astype(jnp.float32), tri_norm_gain, tri_norm_bias).astype(jnp.bfloat16)
    flat_normed = tri_normed.reshape(N * N, C)
    tri_proj = jnp.dot(flat_normed, tri_in_weight, preferred_element_type=jnp.float32).reshape(N, N, 4 * CH)
    left_side = (pair_mask * jax.nn.sigmoid(tri_proj[:, :, :CH]) * tri_proj[:, :, CH:2 * CH]).astype(jnp.bfloat16)
    right_side = (pair_mask * jax.nn.sigmoid(tri_proj[:, :, 2 * CH:3 * CH]) * tri_proj[:, :, 3 * CH:]).astype(jnp.bfloat16)
    tri_gate = jax.nn.sigmoid(jnp.dot(flat_normed, tri_gate_weight, preferred_element_type=jnp.float32)).reshape(N, N, C)
    product = jnp.einsum('ikc,jkc->ijc', left_side.astype(jnp.float32), right_side.astype(jnp.float32))
    product_normed = layer_norm(product, out_norm_gain, out_norm_bias).astype(jnp.bfloat16)
    update = jnp.dot(product_normed.reshape(N * N, CH), tri_out_weight, preferred_element_type=jnp.float32).reshape(N, N, C)
    pair_mid = (pair.astype(jnp.float32) + tri_gate * update).astype(jnp.bfloat16)
    att_normed = layer_norm(pair_mid.astype(jnp.float32), att_norm_gain, att_norm_bias).astype(jnp.bfloat16)
    flat_att = att_normed.reshape(N * N, C)
    projected = jnp.dot(flat_att, qkvg_weight, preferred_element_type=jnp.float32).reshape(N, N, 4, H, DH)
    queries = (projected[:, :, 0] * DH ** (-0.5)).astype(jnp.bfloat16)
    keys = projected[:, :, 1].astype(jnp.bfloat16)
    values = projected[:, :, 2].astype(jnp.bfloat16)
    gate_values = jax.nn.sigmoid(projected[:, :, 3]).reshape(N, N, HD)
    pair_bias = jnp.dot(flat_att, bias_weight, preferred_element_type=jnp.float32).astype(jnp.bfloat16).reshape(N, N, H)
    extra_full = extra_terms(jnp.transpose(pair_bias, (2, 0, 1)), inter_chain, residue_chain, residue_chain, residue_valid)

    def one_column(parts):
        return attend(parts[0], parts[1], parts[2], extra_full)
    results = lax.map(one_column, (jnp.swapaxes(queries, 0, 1), jnp.swapaxes(keys, 0, 1), jnp.swapaxes(values, 0, 1)))
    attended = jnp.swapaxes(results.reshape(N, N, HD), 0, 1)
    gated = (gate_values * attended).astype(jnp.bfloat16)
    final_update = jnp.dot(gated.reshape(N * N, HD), att_out_weight, preferred_element_type=jnp.float32).reshape(N, N, C)
    return (pair_mid.astype(jnp.float32) + pair_mask * final_update).astype(jnp.bfloat16)
```

```python
import functools

import jax
import jax.numpy as jnp
from jax import lax
from jax.experimental import pallas as pl
from jax.experimental.pallas import tpu as pltpu
from jax.sharding import PartitionSpec as P

H = 4
DH = 32
MB = 64

MASK_NEG = 10000.0
EPS = 1e-05
F32 = jnp.float32
BF16 = jnp.bfloat16
VMEM_LIMIT = 48 * 1024 * 1024


def layer_norm(values, gain, shift, axis=-1):
    middle = jnp.mean(values, axis=axis, keepdims=True)
    centred = values - middle
    spread = jnp.mean(centred * centred, axis=axis, keepdims=True)
    return centred * lax.rsqrt(spread + EPS) * gain + shift


def dot_nt(left, right):
    return lax.dot_general(left, right, (((1,), (1,)), ((), ())), preferred_element_type=F32)


def dot_tn(left, right):
    return lax.dot_general(left, right, (((0,), (0,)), ((), ())), preferred_element_type=F32)


def dot_nn(left, right):
    return lax.dot_general(left, right, (((1,), (0,)), ((), ())), preferred_element_type=F32)


def project_kernel(
    pair_ref, valid_i_ref, valid_j_ref, gain_ref, shift_ref, in_t_ref, gate_w_ref, sides_ref, gate_ref
):
    hidden = sides_ref.shape[2]
    normed = layer_norm(pair_ref[0].astype(F32), gain_ref[...], shift_ref[...]).astype(BF16)
    proj = dot_nt(in_t_ref[...], normed)
    mask = valid_i_ref[...] * valid_j_ref[0]
    sides_ref[0, 0] = (mask * jax.nn.sigmoid(proj[:hidden]) * proj[hidden : 2 * hidden]).astype(BF16)
    sides_ref[0, 1] = (
        mask * jax.nn.sigmoid(proj[2 * hidden : 3 * hidden]) * proj[3 * hidden :]
    ).astype(BF16)
    gate_ref[0] = jax.nn.sigmoid(dot_nn(normed, gate_w_ref[...]))


def middle_kernel(
    pair_ref,
    product_ref,
    gate_ref,
    out_gain_ref,
    out_shift_ref,
    out_w_ref,
    att_gain_ref,
    att_shift_ref,
    bias_t_ref,
    mid_ref,
    bias_ref,
):
    normed = layer_norm(
        product_ref[0].astype(F32), out_gain_ref[...], out_shift_ref[...], axis=0
    ).astype(BF16)
    update = dot_tn(normed, out_w_ref[...])
    mid = (pair_ref[0].astype(F32) + gate_ref[0] * update).astype(BF16)
    mid_ref[0] = mid
    att = layer_norm(mid.astype(F32), att_gain_ref[...], att_shift_ref[...]).astype(BF16)
    bias_ref[0] = dot_nt(bias_t_ref[...], att).astype(BF16)


def attention_kernel(
    mid_ref,
    extra_ref,
    valid_i_ref,
    valid_j_ref,
    gain_ref,
    shift_ref,
    qkvg_ref,
    out_w_ref,
    result_ref,
):
    width = H * DH
    mid = mid_ref[0].astype(F32)
    att = layer_norm(mid, gain_ref[...], shift_ref[...]).astype(BF16)
    heads = dot_nn(att, qkvg_ref[...])
    queries = (heads[:, :width] * DH ** (-0.5)).astype(BF16)
    keys = heads[:, width : 2 * width].astype(BF16)
    vals = heads[:, 2 * width : 3 * width].astype(BF16)
    gate = jax.nn.sigmoid(heads[:, 3 * width :])
    attended = []
    for head in range(H):
        lanes = slice(head * DH, (head + 1) * DH)
        scores = dot_nt(queries[:, lanes], keys[:, lanes]) + extra_ref[head]
        powers = jnp.exp(scores - jnp.max(scores, axis=1, keepdims=True))
        total = jnp.sum(powers, axis=1, keepdims=True)
        attended.append(dot_nn(powers.astype(BF16), vals[:, lanes]) / total)
    gated = (gate * jnp.concatenate(attended, axis=1)).astype(BF16)
    update = dot_nn(gated, out_w_ref[...])
    mask = valid_i_ref[...] * valid_j_ref[0]
    result_ref[0] = (mid + mask * update).astype(BF16)


def whole(shape):
    return pl.BlockSpec(shape, lambda c: (0,) * len(shape))


def per_column(shape):
    return pl.BlockSpec((1,) + shape, lambda c: (c,) + (0,) * len(shape))


def column_call(kernel, columns, ins, outs):
    return pl.pallas_call(
        kernel,
        grid=(columns,),
        in_specs=[per_column(a.shape[1:]) if cut else whole(a.shape) for a, cut in ins],
        out_specs=[per_column(shape) for shape, _ in outs],
        out_shape=[jax.ShapeDtypeStruct((columns,) + shape, t) for shape, t in outs],
        compiler_params=pltpu.CompilerParams(vmem_limit_bytes=VMEM_LIMIT),
    )(*[a for a, _ in ins])


def on_device(
    pair,
    block_chain,
    block_valid,
    tri_norm_gain,
    tri_norm_bias,
    tri_in_weight,
    tri_gate_weight,
    out_norm_gain,
    out_norm_bias,
    tri_out_weight,
    att_norm_gain,
    att_norm_bias,
    qkvg_weight,
    bias_weight,
    inter_chain,
    att_out_weight,
):
    row_count, col_count, channels = pair.shape
    hidden = tri_out_weight.shape[0]
    row_devices = lax.axis_size("row")
    residues = row_count * row_devices
    strip = col_count // row_devices
    axes = ("col", "row")
    residue_valid = jnp.repeat(block_valid, MB).astype(F32)
    residue_chain = jnp.repeat(block_chain, MB)
    strip_start = lax.axis_index("col") * col_count + lax.axis_index("row") * strip
    valid_j = lax.dynamic_slice_in_dim(residue_valid, strip_start, strip)[:, None, None]

    own = lax.all_to_all(jnp.swapaxes(pair, 0, 1), "row", split_axis=0, concat_axis=1, tiled=True)
    sides, tri_gate = column_call(
        project_kernel,
        strip,
        [
            (own, True),
            (residue_valid[None, :], False),
            (valid_j, True),
            (tri_norm_gain[None, :], False),
            (tri_norm_bias[None, :], False),
            (tri_in_weight.T, False),
            (tri_gate_weight, False),
        ],
        [((2, hidden, residues), BF16), ((residues, channels), F32)],
    )
    spread = lax.all_to_all(sides, axes, split_axis=2, concat_axis=0, tiled=True)
    product = jnp.einsum(
        "kci,kcj->cji", spread[:, 0], spread[:, 1], preferred_element_type=F32
    ).astype(BF16)
    product = lax.all_to_all(product, axes, split_axis=1, concat_axis=0, tiled=True)
    mid, bias = column_call(
        middle_kernel,
        strip,
        [
            (own, True),
            (jnp.swapaxes(product, 0, 1), True),
            (tri_gate, True),
            (out_norm_gain[:, None], False),
            (out_norm_bias[:, None], False),
            (tri_out_weight, False),
            (att_norm_gain[None, :], False),
            (att_norm_bias[None, :], False),
            (bias_weight.T, False),
        ],
        [((residues, channels), BF16), ((H, residues), BF16)],
    )
    bias = lax.all_gather(bias, axes, axis=0, tiled=True)
    crossing = (residue_chain[:, None] != residue_chain[None, :]).astype(F32)
    extra = (
        jnp.swapaxes(bias, 0, 1).astype(F32)
        + inter_chain[:, None, None] * crossing[None]
        + (MASK_NEG * (residue_valid - 1.0))[None, None, :]
    )
    (result,) = column_call(
        attention_kernel,
        strip,
        [
            (mid, True),
            (extra, False),
            (residue_valid[:, None], False),
            (valid_j, True),
            (att_norm_gain[None, :], False),
            (att_norm_bias[None, :], False),
            (qkvg_weight, False),
            (att_out_weight, False),
        ],
        [((residues, channels), BF16)],
    )
    result = lax.all_to_all(result, "row", split_axis=1, concat_axis=0, tiled=True)
    return jnp.swapaxes(result, 0, 1)


def solution(mesh):
    placed = (P("row", "col", None),) + (P(),) * 15
    return jax.shard_map(
        on_device, mesh=mesh, in_specs=placed, out_specs=P("row", "col", None), check_vma=False
    )
```

```python
import functools

import jax
import jax.numpy as jnp
from jax import lax
from jax.experimental import pallas as pl
from jax.experimental.pallas import tpu as pltpu
from jax.sharding import PartitionSpec as P

H = 4
DH = 32
MB = 64

MASK_NEG = 10000.0
EPS = 1e-05
F32 = jnp.float32
BF16 = jnp.bfloat16
MESH = pl.DeviceIdType.MESH
VMEM_LIMIT = 48 * 1024 * 1024


def layer_norm(values, gain, shift, axis=-1):
    middle = jnp.mean(values, axis=axis, keepdims=True)
    centred = values - middle
    spread = jnp.mean(centred * centred, axis=axis, keepdims=True)
    return centred * lax.rsqrt(spread + EPS) * gain + shift


def dot_nt(left, right):
    return lax.dot_general(left, right, (((1,), (1,)), ((), ())), preferred_element_type=F32)


def dot_tn(left, right):
    return lax.dot_general(left, right, (((0,), (0,)), ((), ())), preferred_element_type=F32)


def dot_nn(left, right):
    return lax.dot_general(left, right, (((1,), (0,)), ((), ())), preferred_element_type=F32)


def project_kernel(pair_ref, mask_ref, gain_ref, shift_ref, in_t_ref, gate_w_ref, sides_ref, gate_ref):
    columns, rows, channels = pair_ref.shape
    flat = pair_ref[...].reshape(columns * rows, channels).astype(F32)
    normed = layer_norm(flat, gain_ref[...], shift_ref[...]).astype(BF16)
    proj = dot_nt(in_t_ref[...], normed)
    half = sides_ref.shape[0]
    sides_ref[...] = (mask_ref[...] * jax.nn.sigmoid(proj[:half]) * proj[half:]).astype(BF16)
    gate = jax.nn.sigmoid(dot_nn(normed, gate_w_ref[...]))
    gate_ref[...] = gate.reshape(columns, rows, channels)


def middle_kernel(
    pair_ref,
    product_ref,
    gate_ref,
    out_gain_ref,
    out_shift_ref,
    out_w_ref,
    att_gain_ref,
    att_shift_ref,
    bias_t_ref,
    mid_ref,
    bias_ref,
):
    columns, rows, channels = pair_ref.shape
    normed = layer_norm(
        product_ref[...].astype(F32), out_gain_ref[...], out_shift_ref[...], axis=0
    ).astype(BF16)
    update = dot_tn(normed, out_w_ref[...])
    flat = pair_ref[...].reshape(columns * rows, channels).astype(F32)
    mid = (flat + gate_ref[...].reshape(columns * rows, channels) * update).astype(BF16)
    mid_ref[...] = mid.reshape(columns, rows, channels)
    att = layer_norm(mid.astype(F32), att_gain_ref[...], att_shift_ref[...]).astype(BF16)
    bias_ref[...] = dot_nt(bias_t_ref[...], att).astype(BF16)


def attention_kernel(
    mid_ref,
    extra_ref,
    valid_i_ref,
    valid_j_ref,
    gain_ref,
    shift_ref,
    qkvg_ref,
    out_w_ref,
    result_ref,
):
    width = H * DH
    mid = mid_ref[0].astype(F32)
    att = layer_norm(mid, gain_ref[...], shift_ref[...]).astype(BF16)
    heads = dot_nn(att, qkvg_ref[...])
    queries = (heads[:, :width] * DH ** (-0.5)).astype(BF16)
    keys = heads[:, width : 2 * width].astype(BF16)
    vals = heads[:, 2 * width : 3 * width].astype(BF16)
    gate = jax.nn.sigmoid(heads[:, 3 * width :])
    attended = []
    for head in range(H):
        lanes = slice(head * DH, (head + 1) * DH)
        scores = dot_nt(queries[:, lanes], keys[:, lanes]) + extra_ref[head]
        powers = jnp.exp(scores - jnp.max(scores, axis=1, keepdims=True))
        total = jnp.sum(powers, axis=1, keepdims=True)
        attended.append(dot_nn(powers.astype(BF16), vals[:, lanes]) / total)
    gated = (gate * jnp.concatenate(attended, axis=1)).astype(BF16)
    update = dot_nn(gated, out_w_ref[...])
    mask = valid_i_ref[...] * valid_j_ref[0]
    result_ref[0] = (mid + mask * update).astype(BF16)


def greet(peers):
    barrier = pltpu.get_barrier_semaphore()
    for peer in peers:
        pl.semaphore_signal(barrier, inc=1, device_id=peer, device_id_type=MESH)
    pl.semaphore_wait(barrier, len(peers))


def gather_kernel(nr, nq, src, out, own_sem, col_send, col_recv, row_send, row_recv):
    r, q = lax.axis_index("row"), lax.axis_index("col")
    row_peers = [(lax.rem(r + e, nr), q) for e in range(1, nr)]
    col_peers = [(r, lax.rem(q + d, nq)) for d in range(1, nq)]
    greet(row_peers + col_peers)
    own = pltpu.make_async_copy(src, out.at[q, r], own_sem)
    own.start()
    over_col = []
    for d in range(1, nq):
        over_col.append(
            pltpu.make_async_remote_copy(
                src_ref=src,
                dst_ref=out.at[q, r],
                send_sem=col_send.at[d - 1],
                recv_sem=col_recv.at[d - 1],
                device_id=col_peers[d - 1],
                device_id_type=MESH,
            )
        )
        over_col[-1].start()
    over_row = []
    for d in range(nq):
        source = lax.rem(q + nq - d, nq)
        block = src if d == 0 else out.at[source, r]
        if d > 0:
            over_col[d - 1].wait_recv()
        for e in range(1, nr):
            over_row.append(
                pltpu.make_async_remote_copy(
                    src_ref=block,
                    dst_ref=out.at[source, r],
                    send_sem=row_send.at[e - 1, d],
                    recv_sem=row_recv.at[e - 1, d],
                    device_id=row_peers[e - 1],
                    device_id_type=MESH,
                )
            )
            over_row[-1].start()
    own.wait()
    for copy in over_row:
        copy.wait_recv()
    for copy in over_col + over_row:
        copy.wait_send()


def gather_all(block, nr, nq):
    return pl.pallas_call(
        functools.partial(gather_kernel, nr, nq),
        out_shape=jax.ShapeDtypeStruct((nq, nr) + block.shape, block.dtype),
        in_specs=[pl.BlockSpec(memory_space=pltpu.VMEM)],
        out_specs=pl.BlockSpec(memory_space=pltpu.VMEM),
        scratch_shapes=[
            pltpu.SemaphoreType.DMA,
            pltpu.SemaphoreType.DMA((nq - 1,)),
            pltpu.SemaphoreType.DMA((nq - 1,)),
            pltpu.SemaphoreType.DMA((nr - 1, nq)),
            pltpu.SemaphoreType.DMA((nr - 1, nq)),
        ],
        compiler_params=pltpu.CompilerParams(
            collective_id=0, has_side_effects=True, vmem_limit_bytes=VMEM_LIMIT
        ),
    )(block)


def swap_kernel(nr, gathers_rows, src, out, own_sem, send, recv):
    r, q = lax.axis_index("row"), lax.axis_index("col")
    peers = [(lax.rem(r + e, nr), q) for e in range(1, nr)]
    greet(peers)

    def outgoing(partner):
        return src.at[partner] if gathers_rows else src.at[:, partner]

    landing = out.at[:, r] if gathers_rows else out.at[r]
    copies = []
    for e in range(1, nr):
        copies.append(
            pltpu.make_async_remote_copy(
                src_ref=outgoing(peers[e - 1][0]),
                dst_ref=landing,
                send_sem=send.at[e - 1],
                recv_sem=recv.at[e - 1],
                device_id=peers[e - 1],
                device_id_type=MESH,
            )
        )
        copies[-1].start()
    own = pltpu.make_async_copy(outgoing(r), landing, own_sem)
    own.start()
    own.wait()
    for copy in copies:
        copy.wait()


def swap_rows(array, nr, gathers_rows):
    shape = (array.shape[1], array.shape[0]) + array.shape[2:]
    return pl.pallas_call(
        functools.partial(swap_kernel, nr, gathers_rows),
        out_shape=jax.ShapeDtypeStruct(shape, array.dtype),
        in_specs=[pl.BlockSpec(memory_space=pltpu.VMEM)],
        out_specs=pl.BlockSpec(memory_space=pltpu.VMEM),
        scratch_shapes=[
            pltpu.SemaphoreType.DMA,
            pltpu.SemaphoreType.DMA((nr - 1,)),
            pltpu.SemaphoreType.DMA((nr - 1,)),
        ],
        compiler_params=pltpu.CompilerParams(
            collective_id=1 if gathers_rows else 2,
            has_side_effects=True,
            vmem_limit_bytes=VMEM_LIMIT,
        ),
    )(array)


def step_call(kernel, steps, ins, outs):
    def spec(shape, dim):
        block = tuple(n // steps if d == dim else n for d, n in enumerate(shape))
        return pl.BlockSpec(block, lambda c: tuple(c if d == dim else 0 for d in range(len(shape))))

    return pl.pallas_call(
        kernel,
        grid=(steps,),
        in_specs=[spec(a.shape, dim) for a, dim in ins],
        out_specs=[spec(shape, dim) for shape, _, dim in outs],
        out_shape=[jax.ShapeDtypeStruct(shape, t) for shape, t, _ in outs],
        compiler_params=pltpu.CompilerParams(vmem_limit_bytes=VMEM_LIMIT),
    )(*[a for a, _ in ins])


def on_device(
    pair,
    block_chain,
    block_valid,
    tri_norm_gain,
    tri_norm_bias,
    tri_in_weight,
    tri_gate_weight,
    out_norm_gain,
    out_norm_bias,
    tri_out_weight,
    att_norm_gain,
    att_norm_bias,
    qkvg_weight,
    bias_weight,
    inter_chain,
    att_out_weight,
):
    row_count, col_count, channels = pair.shape
    hidden = tri_out_weight.shape[0]
    row_devices = lax.axis_size("row")
    col_devices = lax.axis_size("col")
    devices = row_devices * col_devices
    residues = row_count * row_devices
    strip = col_count // row_devices
    axes = ("col", "row")
    residue_valid = jnp.repeat(block_valid, MB).astype(F32)
    residue_chain = jnp.repeat(block_chain, MB)
    strip_start = lax.axis_index("col") * col_count + lax.axis_index("row") * strip
    valid_j = lax.dynamic_slice_in_dim(residue_valid, strip_start, strip)[:, None]

    share = hidden // devices
    flat = strip * residues
    steps = strip // 2 if strip % 2 == 0 else 1
    by_column = jnp.swapaxes(pair, 0, 1).reshape(row_devices, strip, row_count, channels)
    own = swap_rows(by_column, row_devices, True).reshape(strip, residues, channels)
    in_t = (
        tri_in_weight.reshape(channels, 2, 2, devices, share)
        .transpose(2, 3, 1, 4, 0)
        .reshape(4 * hidden, channels)
    )
    mask = (valid_j * residue_valid[None, :]).reshape(1, flat)
    sides, tri_gate = step_call(
        project_kernel,
        steps,
        [
            (own, 0),
            (mask, 1),
            (tri_norm_gain[None, :], None),
            (tri_norm_bias[None, :], None),
            (in_t, None),
            (tri_gate_weight, None),
        ],
        [((2 * hidden, flat), BF16, 1), ((strip, residues, channels), F32, 0)],
    )
    spread = lax.all_to_all(
        sides.reshape(devices, 2 * share, flat), axes, split_axis=0, concat_axis=0, tiled=True
    ).reshape(devices, 2, share, strip, residues)
    product = jnp.einsum(
        "pcki,pckj->cji", spread[:, 0], spread[:, 1], preferred_element_type=F32
    ).astype(BF16)
    product = jnp.swapaxes(product.reshape(share, devices, flat), 0, 1)
    product = lax.all_to_all(product, axes, split_axis=0, concat_axis=0, tiled=True)
    mid, bias = step_call(
        middle_kernel,
        steps,
        [
            (own, 0),
            (product.reshape(hidden, flat), 1),
            (tri_gate, 0),
            (out_norm_gain[:, None], None),
            (out_norm_bias[:, None], None),
            (tri_out_weight, None),
            (att_norm_gain[None, :], None),
            (att_norm_bias[None, :], None),
            (bias_weight.T, None),
        ],
        [((strip, residues, channels), BF16, 0), ((H, flat), BF16, 1)],
    )
    bias = gather_all(bias, row_devices, col_devices).reshape(devices, H, strip, residues)
    bias = jnp.swapaxes(bias, 0, 1).reshape(H, residues, residues)
    crossing = (residue_chain[:, None] != residue_chain[None, :]).astype(F32)
    extra = (
        bias.astype(F32)
        + inter_chain[:, None, None] * crossing[None]
        + (MASK_NEG * (residue_valid - 1.0))[None, None, :]
    )
    (result,) = step_call(
        attention_kernel,
        strip,
        [
            (mid, 0),
            (extra, None),
            (residue_valid[:, None], None),
            (valid_j[:, :, None], 0),
            (att_norm_gain[None, :], None),
            (att_norm_bias[None, :], None),
            (qkvg_weight, None),
            (att_out_weight, None),
        ],
        [((strip, residues, channels), BF16, 0)],
    )
    result = swap_rows(
        result.reshape(strip, row_devices, row_count, channels), row_devices, False
    ).reshape(col_count, row_count, channels)
    return jnp.swapaxes(result, 0, 1)


def solution(mesh):
    placed = (P("row", "col", None),) + (P(),) * 15
    return jax.shard_map(
        on_device, mesh=mesh, in_specs=placed, out_specs=P("row", "col", None), check_vma=False
    )
```

```python
import functools

import jax
import jax.numpy as jnp
from jax import lax
from jax.experimental import pallas as pl
from jax.experimental.pallas import tpu as pltpu
from jax.sharding import PartitionSpec as P

H = 4
DH = 32
MB = 64

MASK_NEG = 10000.0
EPS = 1e-05
FILLED = -1e30
F32 = jnp.float32
BF16 = jnp.bfloat16
MESH = pl.DeviceIdType.MESH
VMEM_LIMIT = 48 * 1024 * 1024


def layer_norm(values, gain, shift, axis=-1):
    middle = jnp.mean(values, axis=axis, keepdims=True)
    centred = values - middle
    spread = jnp.mean(centred * centred, axis=axis, keepdims=True)
    return centred * lax.rsqrt(spread + EPS) * gain + shift


def dot_nt(left, right):
    return lax.dot_general(left, right, (((1,), (1,)), ((), ())), preferred_element_type=F32)


def dot_tn(left, right):
    return lax.dot_general(left, right, (((0,), (0,)), ((), ())), preferred_element_type=F32)


def dot_nn(left, right):
    return lax.dot_general(left, right, (((1,), (0,)), ((), ())), preferred_element_type=F32)


def project_kernel(pair_ref, mask_ref, gain_ref, shift_ref, in_t_ref, sides_ref):
    columns, rows, channels = pair_ref.shape
    flat = pair_ref[...].reshape(columns * rows, channels).astype(F32)
    normed = layer_norm(flat, gain_ref[...], shift_ref[...]).astype(BF16)
    proj = dot_nt(in_t_ref[...], normed)
    half = sides_ref.shape[0]
    sides_ref[...] = (mask_ref[...] * jax.nn.sigmoid(proj[:half]) * proj[half:]).astype(BF16)


def gate_kernel(pair_ref, gain_ref, shift_ref, gate_w_ref, gate_ref):
    columns, rows, channels = pair_ref.shape
    flat = pair_ref[...].reshape(columns * rows, channels).astype(F32)
    normed = layer_norm(flat, gain_ref[...], shift_ref[...]).astype(BF16)
    gate = jax.nn.sigmoid(dot_nn(normed, gate_w_ref[...]))
    gate_ref[...] = gate.reshape(columns, rows, channels)


def middle_kernel(
    pair_ref,
    product_ref,
    gate_ref,
    out_gain_ref,
    out_shift_ref,
    out_w_ref,
    att_gain_ref,
    att_shift_ref,
    bias_t_ref,
    mid_ref,
    bias_ref,
):
    columns, rows, channels = pair_ref.shape
    normed = layer_norm(
        product_ref[...].astype(F32), out_gain_ref[...], out_shift_ref[...], axis=0
    ).astype(BF16)
    update = dot_tn(normed, out_w_ref[...])
    flat = pair_ref[...].reshape(columns * rows, channels).astype(F32)
    mid = (flat + gate_ref[...].reshape(columns * rows, channels) * update).astype(BF16)
    mid_ref[...] = mid.reshape(columns, rows, channels)
    att = layer_norm(mid.astype(F32), att_gain_ref[...], att_shift_ref[...]).astype(BF16)
    bias = dot_nt(bias_t_ref[...], att).astype(BF16)
    for column in range(columns):
        bias_ref[column] = bias[:, column * rows : (column + 1) * rows]


def stack_rows(parts):
    return jnp.concatenate([part for part in parts if part.shape[0]], axis=0)


def attention_kernel(
    mid_ref,
    extra_ref,
    valid_i_ref,
    valid_j_ref,
    gain_ref,
    shift_ref,
    qkvg_ref,
    out_w_ref,
    result_ref,
):
    width = H * DH
    mid = mid_ref[0].astype(F32)
    att = layer_norm(mid, gain_ref[...], shift_ref[...]).astype(BF16)
    heads = dot_nn(att, qkvg_ref[...])
    queries = (heads[:, :width] * DH ** (-0.5)).astype(BF16)
    keys = heads[:, width : 2 * width].astype(BF16)
    vals = heads[:, 2 * width : 3 * width].astype(BF16)
    gate = jax.nn.sigmoid(heads[:, 3 * width :])
    rows, padded = extra_ref.shape[1:]
    lane_head = lax.broadcasted_iota(jnp.int32, (rows, width), 1) // DH
    filler = jnp.zeros((padded - rows, width), BF16)
    key_rows, val_rows, one_rows = [], [], []
    for head in range(H):
        inside = (lane_head == head).astype(F32).astype(BF16)
        key_rows += [keys * inside, filler]
        val_rows += [vals * inside, filler]
        one_rows += [inside, filler]
    scores = dot_nt(queries, stack_rows(key_rows))
    powers = []
    for head in range(H):
        part = scores[:, head * padded : (head + 1) * padded] + extra_ref[head]
        powers.append(jnp.exp(part - jnp.max(part, axis=1, keepdims=True)).astype(BF16))
    sums = dot_nn(
        jnp.concatenate(powers, axis=1),
        jnp.concatenate([stack_rows(val_rows), stack_rows(one_rows)], axis=1),
    )
    gated = (gate * sums[:, :width] / sums[:, width:]).astype(BF16)
    update = dot_nn(gated, out_w_ref[...])
    mask = valid_i_ref[...] * valid_j_ref[0]
    result_ref[0] = (mid + mask * update).astype(BF16)


def greet(peers):
    barrier = pltpu.get_barrier_semaphore()
    for peer in peers:
        pl.semaphore_signal(barrier, inc=1, device_id=peer, device_id_type=MESH)
    pl.semaphore_wait(barrier, len(peers))


def gather_kernel(nr, nq, src, out, own_sem, col_send, col_recv, row_send, row_recv):
    r, q = lax.axis_index("row"), lax.axis_index("col")
    row_peers = [(lax.rem(r + e, nr), q) for e in range(1, nr)]
    col_peers = [(r, lax.rem(q + d, nq)) for d in range(1, nq)]
    greet(row_peers + col_peers)
    own = pltpu.make_async_copy(src, out.at[q, r], own_sem)
    own.start()
    over_col = []
    for d in range(1, nq):
        over_col.append(
            pltpu.make_async_remote_copy(
                src_ref=src,
                dst_ref=out.at[q, r],
                send_sem=col_send.at[d - 1],
                recv_sem=col_recv.at[d - 1],
                device_id=col_peers[d - 1],
                device_id_type=MESH,
            )
        )
        over_col[-1].start()
    over_row = []
    for d in range(nq):
        source = lax.rem(q + nq - d, nq)
        block = src if d == 0 else out.at[source, r]
        if d > 0:
            over_col[d - 1].wait_recv()
        for e in range(1, nr):
            over_row.append(
                pltpu.make_async_remote_copy(
                    src_ref=block,
                    dst_ref=out.at[source, r],
                    send_sem=row_send.at[e - 1, d],
                    recv_sem=row_recv.at[e - 1, d],
                    device_id=row_peers[e - 1],
                    device_id_type=MESH,
                )
            )
            over_row[-1].start()
    own.wait()
    for copy in over_row:
        copy.wait_recv()
    for copy in over_col + over_row:
        copy.wait_send()


def gather_all(block, nr, nq):
    return pl.pallas_call(
        functools.partial(gather_kernel, nr, nq),
        out_shape=jax.ShapeDtypeStruct((nq, nr) + block.shape, block.dtype),
        in_specs=[pl.BlockSpec(memory_space=pltpu.VMEM)],
        out_specs=pl.BlockSpec(memory_space=pltpu.VMEM),
        scratch_shapes=[
            pltpu.SemaphoreType.DMA,
            pltpu.SemaphoreType.DMA((nq - 1,)),
            pltpu.SemaphoreType.DMA((nq - 1,)),
            pltpu.SemaphoreType.DMA((nr - 1, nq)),
            pltpu.SemaphoreType.DMA((nr - 1, nq)),
        ],
        compiler_params=pltpu.CompilerParams(
            collective_id=0, has_side_effects=True, vmem_limit_bytes=VMEM_LIMIT
        ),
    )(block)


def swap_kernel(nr, src, out, own_sem, send, recv):
    r, q = lax.axis_index("row"), lax.axis_index("col")
    peers = [(lax.rem(r + e, nr), q) for e in range(1, nr)]
    greet(peers)
    copies = []
    for e in range(1, nr):
        copies.append(
            pltpu.make_async_remote_copy(
                src_ref=src.at[:, peers[e - 1][0]],
                dst_ref=out.at[r],
                send_sem=send.at[e - 1],
                recv_sem=recv.at[e - 1],
                device_id=peers[e - 1],
                device_id_type=MESH,
            )
        )
        copies[-1].start()
    own = pltpu.make_async_copy(src.at[:, r], out.at[r], own_sem)
    own.start()
    own.wait()
    for copy in copies:
        copy.wait()


def swap_rows(array, nr):
    shape = (array.shape[1], array.shape[0]) + array.shape[2:]
    return pl.pallas_call(
        functools.partial(swap_kernel, nr),
        out_shape=jax.ShapeDtypeStruct(shape, array.dtype),
        in_specs=[pl.BlockSpec(memory_space=pltpu.VMEM)],
        out_specs=pl.BlockSpec(memory_space=pltpu.VMEM),
        scratch_shapes=[
            pltpu.SemaphoreType.DMA,
            pltpu.SemaphoreType.DMA((nr - 1,)),
            pltpu.SemaphoreType.DMA((nr - 1,)),
        ],
        compiler_params=pltpu.CompilerParams(
            collective_id=2, has_side_effects=True, vmem_limit_bytes=VMEM_LIMIT
        ),
    )(array)


def spread_kernel(nr, nq, sides, pair, spread, strip, own_sem, send, recv, row_send, row_recv):
    r, q = lax.axis_index("row"), lax.axis_index("col")
    devices = nr * nq
    me = q * nr + r
    others = [lax.rem(me + d, devices) for d in range(1, devices)]
    places = [(lax.rem(other, nr), other // nr) for other in others]
    greet(places)
    copies = []
    for d in range(devices - 1):
        copies.append(
            pltpu.make_async_remote_copy(
                src_ref=sides.at[others[d]],
                dst_ref=spread.at[me],
                send_sem=send.at[d],
                recv_sem=recv.at[d],
                device_id=places[d],
                device_id_type=MESH,
            )
        )
        copies[-1].start()
    for e in range(1, nr):
        partner = lax.rem(r + e, nr)
        copies.append(
            pltpu.make_async_remote_copy(
                src_ref=pair.at[partner],
                dst_ref=strip.at[:, r],
                send_sem=row_send.at[e - 1],
                recv_sem=row_recv.at[e - 1],
                device_id=(partner, q),
                device_id_type=MESH,
            )
        )
        copies[-1].start()
    own = [
        pltpu.make_async_copy(sides.at[me], spread.at[me], own_sem.at[0]),
        pltpu.make_async_copy(pair.at[r], strip.at[:, r], own_sem.at[1]),
    ]
    for copy in own:
        copy.start()
    for copy in own:
        copy.wait()
    for copy in copies:
        copy.wait()


def spread_all(sides, pair, nr, nq):
    shape = (pair.shape[1], pair.shape[0]) + pair.shape[2:]
    return pl.pallas_call(
        functools.partial(spread_kernel, nr, nq),
        out_shape=[
            jax.ShapeDtypeStruct(sides.shape, sides.dtype),
            jax.ShapeDtypeStruct(shape, pair.dtype),
        ],
        in_specs=[pl.BlockSpec(memory_space=pltpu.VMEM)] * 2,
        out_specs=[pl.BlockSpec(memory_space=pltpu.VMEM)] * 2,
        scratch_shapes=[
            pltpu.SemaphoreType.DMA((2,)),
            pltpu.SemaphoreType.DMA((nr * nq - 1,)),
            pltpu.SemaphoreType.DMA((nr * nq - 1,)),
            pltpu.SemaphoreType.DMA((nr - 1,)),
            pltpu.SemaphoreType.DMA((nr - 1,)),
        ],
        compiler_params=pltpu.CompilerParams(
            collective_id=1, has_side_effects=True, vmem_limit_bytes=VMEM_LIMIT
        ),
    )(sides, pair)


def step_call(kernel, steps, ins, outs):
    def spec(shape, dim):
        block = tuple(n // steps if d == dim else n for d, n in enumerate(shape))
        return pl.BlockSpec(block, lambda c: tuple(c if d == dim else 0 for d in range(len(shape))))

    return pl.pallas_call(
        kernel,
        grid=(steps,),
        in_specs=[spec(a.shape, dim) for a, dim in ins],
        out_specs=[spec(shape, dim) for shape, _, dim in outs],
        out_shape=[jax.ShapeDtypeStruct(shape, t) for shape, t, _ in outs],
        compiler_params=pltpu.CompilerParams(vmem_limit_bytes=VMEM_LIMIT),
    )(*[a for a, _ in ins])


def on_device(
    pair,
    block_chain,
    block_valid,
    tri_norm_gain,
    tri_norm_bias,
    tri_in_weight,
    tri_gate_weight,
    out_norm_gain,
    out_norm_bias,
    tri_out_weight,
    att_norm_gain,
    att_norm_bias,
    qkvg_weight,
    bias_weight,
    inter_chain,
    att_out_weight,
):
    row_count, col_count, channels = pair.shape
    hidden = tri_out_weight.shape[0]
    row_devices = lax.axis_size("row")
    col_devices = lax.axis_size("col")
    devices = row_devices * col_devices
    residues = row_count * row_devices
    strip = col_count // row_devices
    axes = ("col", "row")
    residue_valid = jnp.repeat(block_valid, MB).astype(F32)
    residue_chain = jnp.repeat(block_chain, MB)
    strip_start = lax.axis_index("col") * col_count + lax.axis_index("row") * strip
    valid_j = lax.dynamic_slice_in_dim(residue_valid, strip_start, strip)[:, None]

    share = hidden // devices
    flat = strip * residues
    steps = strip // 2 if strip % 2 == 0 else 1
    by_column = jnp.swapaxes(pair, 0, 1)
    in_t = (
        tri_in_weight.reshape(channels, 2, 2, devices, share)
        .transpose(2, 3, 1, 4, 0)
        .reshape(4 * hidden, channels)
    )
    valid_rows = lax.dynamic_slice_in_dim(
        residue_valid, lax.axis_index("row") * row_count, row_count
    )
    valid_cols = lax.dynamic_slice_in_dim(
        residue_valid, lax.axis_index("col") * col_count, col_count
    )
    mask = (valid_cols[:, None] * valid_rows[None, :]).reshape(1, flat)
    (sides,) = step_call(
        project_kernel,
        steps,
        [
            (by_column, 0),
            (mask, 1),
            (tri_norm_gain[None, :], None),
            (tri_norm_bias[None, :], None),
            (in_t, None),
        ],
        [((2 * hidden, flat), BF16, 1)],
    )
    spread, own = spread_all(
        sides.reshape(devices, 2 * share, flat),
        by_column.reshape(row_devices, strip, row_count, channels),
        row_devices,
        col_devices,
    )
    own = own.reshape(strip, residues, channels)
    (tri_gate,) = step_call(
        gate_kernel,
        steps,
        [
            (own, 0),
            (tri_norm_gain[None, :], None),
            (tri_norm_bias[None, :], None),
            (tri_gate_weight, None),
        ],
        [((strip, residues, channels), F32, 0)],
    )
    spread = (
        spread.reshape(col_devices, row_devices, 2, share, col_count, row_count)
        .transpose(2, 3, 0, 4, 1, 5)
        .reshape(2, share, residues, residues)
    )
    product = jnp.einsum(
        "cki,ckj->cji", spread[0], spread[1], preferred_element_type=F32
    ).astype(BF16)
    product = jnp.swapaxes(product.reshape(share, devices, flat), 0, 1)
    product = lax.all_to_all(product, axes, split_axis=0, concat_axis=0, tiled=True)
    mid, bias = step_call(
        middle_kernel,
        steps,
        [
            (own, 0),
            (product.reshape(hidden, flat), 1),
            (tri_gate, 0),
            (out_norm_gain[:, None], None),
            (out_norm_bias[:, None], None),
            (tri_out_weight, None),
            (att_norm_gain[None, :], None),
            (att_norm_bias[None, :], None),
            (bias_weight.T, None),
        ],
        [((strip, residues, channels), BF16, 0), ((strip, H, residues), BF16, 0)],
    )
    bias = gather_all(bias, row_devices, col_devices).reshape(residues, H, residues)
    crossing = (residue_chain[:, None] != residue_chain[None, :]).astype(F32)
    extra = (
        jnp.swapaxes(bias, 0, 1).astype(F32)
        + inter_chain[:, None, None] * crossing[None]
        + (MASK_NEG * (residue_valid - 1.0))[None, None, :]
    )
    extra = jnp.pad(extra, ((0, 0), (0, 0), (0, -residues % 128)), constant_values=FILLED)
    (result,) = step_call(
        attention_kernel,
        strip,
        [
            (mid, 0),
            (extra, None),
            (residue_valid[:, None], None),
            (valid_j[:, :, None], 0),
            (att_norm_gain[None, :], None),
            (att_norm_bias[None, :], None),
            (qkvg_weight, None),
            (att_out_weight, None),
        ],
        [((strip, residues, channels), BF16, 0)],
    )
    result = swap_rows(
        result.reshape(strip, row_devices, row_count, channels), row_devices
    ).reshape(col_count, row_count, channels)
    return jnp.swapaxes(result, 0, 1)


def solution(mesh):
    placed = (P("row", "col", None),) + (P(),) * 15
    return jax.shard_map(
        on_device, mesh=mesh, in_specs=placed, out_specs=P("row", "col", None), check_vma=False
    )
```

```python
import functools

import jax
import jax.numpy as jnp
from jax import lax
from jax.experimental import pallas as pl
from jax.experimental.pallas import tpu as pltpu
from jax.sharding import PartitionSpec as P

H = 4
DH = 32
MB = 64

MASK_NEG = 10000.0
EPS = 1e-05
FILLED = -1e30
F32 = jnp.float32
BF16 = jnp.bfloat16
MESH = pl.DeviceIdType.MESH
VMEM_LIMIT = 48 * 1024 * 1024


def layer_norm(values, gain, shift, axis=-1):
    middle = jnp.mean(values, axis=axis, keepdims=True)
    centred = values - middle
    spread = jnp.mean(centred * centred, axis=axis, keepdims=True)
    return centred * lax.rsqrt(spread + EPS) * gain + shift


def dot_nt(left, right):
    return lax.dot_general(left, right, (((1,), (1,)), ((), ())), preferred_element_type=F32)


def dot_tn(left, right):
    return lax.dot_general(left, right, (((0,), (0,)), ((), ())), preferred_element_type=F32)


def dot_nn(left, right):
    return lax.dot_general(left, right, (((1,), (0,)), ((), ())), preferred_element_type=F32)


def project_kernel(pair_ref, mask_ref, gain_ref, shift_ref, in_t_ref, sides_ref):
    columns, rows, channels = pair_ref.shape
    flat = pair_ref[...].reshape(columns * rows, channels).astype(F32)
    normed = layer_norm(flat, gain_ref[...], shift_ref[...]).astype(BF16)
    proj = dot_nt(in_t_ref[...], normed)
    half = sides_ref.shape[0]
    sides_ref[...] = (mask_ref[...] * jax.nn.sigmoid(proj[:half]) * proj[half:]).astype(BF16)


def gate_kernel(pair_ref, gain_ref, shift_ref, gate_w_ref, gate_ref):
    columns, rows, channels = pair_ref.shape
    flat = pair_ref[...].reshape(columns * rows, channels).astype(F32)
    normed = layer_norm(flat, gain_ref[...], shift_ref[...]).astype(BF16)
    gate = jax.nn.sigmoid(dot_nn(normed, gate_w_ref[...]))
    gate_ref[...] = gate.reshape(columns, rows, channels)


def middle_kernel(
    pair_ref,
    product_ref,
    gate_ref,
    out_gain_ref,
    out_shift_ref,
    out_w_ref,
    att_gain_ref,
    att_shift_ref,
    bias_t_ref,
    mid_ref,
    bias_ref,
):
    columns, rows, channels = pair_ref.shape
    normed = layer_norm(
        product_ref[...].astype(F32), out_gain_ref[...], out_shift_ref[...], axis=0
    ).astype(BF16)
    update = dot_tn(normed, out_w_ref[...])
    flat = pair_ref[...].reshape(columns * rows, channels).astype(F32)
    mid = (flat + gate_ref[...].reshape(columns * rows, channels) * update).astype(BF16)
    mid_ref[...] = mid.reshape(columns, rows, channels)
    att = layer_norm(mid.astype(F32), att_gain_ref[...], att_shift_ref[...]).astype(BF16)
    bias = dot_nt(bias_t_ref[...], att).astype(BF16)
    for column in range(columns):
        bias_ref[column] = bias[:, column * rows : (column + 1) * rows]


def stack_rows(parts):
    return jnp.concatenate([part for part in parts if part.shape[0]], axis=0)


def attention_kernel(
    nr,
    columns,
    mid_ref,
    extra_ref,
    valid_i_ref,
    valid_j_ref,
    gain_ref,
    shift_ref,
    qkvg_ref,
    out_w_ref,
    out,
    result,
    own_sem,
    send,
    recv,
):
    column = pl.program_id(0)
    r, q = lax.axis_index("row"), lax.axis_index("col")
    peers = [(lax.rem(r + e, nr), q) for e in range(1, nr)]
    barrier = pltpu.get_barrier_semaphore()

    def copies(c):
        return [
            pltpu.make_async_remote_copy(
                src_ref=result.at[c, peer[0]],
                dst_ref=out.at[r, c],
                send_sem=send.at[e, c],
                recv_sem=recv.at[e, c],
                device_id=peer,
                device_id_type=MESH,
            )
            for e, peer in enumerate(peers)
        ] + [pltpu.make_async_copy(result.at[c, r], out.at[r, c], own_sem.at[c])]

    @pl.when(column == 0)
    def _():
        for peer in peers:
            pl.semaphore_signal(barrier, inc=1, device_id=peer, device_id_type=MESH)

    width = H * DH
    mid = mid_ref[0].astype(F32)
    att = layer_norm(mid, gain_ref[...], shift_ref[...]).astype(BF16)
    heads = dot_nn(att, qkvg_ref[...])
    queries = (heads[:, :width] * DH ** (-0.5)).astype(BF16)
    keys = heads[:, width : 2 * width].astype(BF16)
    vals = heads[:, 2 * width : 3 * width].astype(BF16)
    gate = jax.nn.sigmoid(heads[:, 3 * width :])
    rows, padded = extra_ref.shape[1:]
    lane_head = lax.broadcasted_iota(jnp.int32, (rows, width), 1) // DH
    filler = jnp.zeros((padded - rows, width), BF16)
    key_rows, val_rows, one_rows = [], [], []
    for head in range(H):
        inside = (lane_head == head).astype(F32).astype(BF16)
        key_rows += [keys * inside, filler]
        val_rows += [vals * inside, filler]
        one_rows += [inside, filler]
    scores = dot_nt(queries, stack_rows(key_rows))
    powers = []
    for head in range(H):
        part = scores[:, head * padded : (head + 1) * padded] + extra_ref[head]
        powers.append(jnp.exp(part - jnp.max(part, axis=1, keepdims=True)).astype(BF16))
    sums = dot_nn(
        jnp.concatenate(powers, axis=1),
        jnp.concatenate([stack_rows(val_rows), stack_rows(one_rows)], axis=1),
    )
    gated = (gate * sums[:, :width] / sums[:, width:]).astype(BF16)
    update = dot_nn(gated, out_w_ref[...])
    mask = valid_i_ref[...] * valid_j_ref[0]
    rows = mid.shape[0] // nr
    result[column] = (mid + mask * update).astype(BF16).reshape(nr, rows, mid.shape[1])

    @pl.when(column == 0)
    def _():
        pl.semaphore_wait(barrier, len(peers))

    for copy in copies(column):
        copy.start()

    @pl.when(column == columns - 1)
    def _():
        for c in range(columns):
            for copy in copies(c):
                copy.wait()


def greet(peers):
    barrier = pltpu.get_barrier_semaphore()
    for peer in peers:
        pl.semaphore_signal(barrier, inc=1, device_id=peer, device_id_type=MESH)
    pl.semaphore_wait(barrier, len(peers))


def gather_kernel(
    nr, nq, src, out, own_sem, col_send, col_recv, row_send, row_recv, mate_send, mate_recv
):
    r, q = lax.axis_index("row"), lax.axis_index("col")
    row_peers = [(lax.rem(r + e, nr), q) for e in range(1, nr)]
    col_peers = [(r, lax.rem(q + 2 * d, nq)) for d in range(1, nq // 2)]
    mate = (r, q + 1 - 2 * lax.rem(q, 2))
    greet(row_peers + col_peers + [mate])

    def send(block, place, send_sem, recv_sem, peer):
        copy = pltpu.make_async_remote_copy(
            src_ref=block,
            dst_ref=out.at[place[0], place[1]],
            send_sem=send_sem,
            recv_sem=recv_sem,
            device_id=peer,
            device_id_type=MESH,
        )
        copy.start()
        return copy

    over_col = [
        send(src, (q, r), col_send.at[d], col_recv.at[d], peer) for d, peer in enumerate(col_peers)
    ]
    own = pltpu.make_async_copy(src, out.at[q, r], own_sem)
    own.start()
    over_row, to_mate = [], []
    for d in range(nq // 2):
        source = lax.rem(q + nq - 2 * d, nq)
        block = src if d == 0 else out.at[source, r]
        if d > 0:
            over_col[d - 1].wait_recv()
        over_row.append(
            [
                send(block, (source, r), row_send.at[e, d], row_recv.at[e, d], peer)
                for e, peer in enumerate(row_peers)
            ]
        )
        to_mate.append(send(block, (source, r), mate_send.at[0, d], mate_recv.at[0, d], mate))
    for d in range(nq // 2):
        source = lax.rem(q + nq - 2 * d, nq)
        for e in range(nr - 1):
            over_row[d][e].wait_recv()
            place = (source, lax.rem(r + nr - 1 - e, nr))
            to_mate.append(
                send(
                    out.at[place[0], place[1]],
                    place,
                    mate_send.at[e + 1, d],
                    mate_recv.at[e + 1, d],
                    mate,
                )
            )
    own.wait()
    for copy in to_mate:
        copy.wait()
    for copy in over_col + sum(over_row, []):
        copy.wait_send()


def gather_all(block, nr, nq):
    return pl.pallas_call(
        functools.partial(gather_kernel, nr, nq),
        out_shape=jax.ShapeDtypeStruct((nq, nr) + block.shape, block.dtype),
        in_specs=[pl.BlockSpec(memory_space=pltpu.VMEM)],
        out_specs=pl.BlockSpec(memory_space=pltpu.VMEM),
        scratch_shapes=[
            pltpu.SemaphoreType.DMA,
            pltpu.SemaphoreType.DMA((nq // 2 - 1,)),
            pltpu.SemaphoreType.DMA((nq // 2 - 1,)),
            pltpu.SemaphoreType.DMA((nr - 1, nq // 2)),
            pltpu.SemaphoreType.DMA((nr - 1, nq // 2)),
            pltpu.SemaphoreType.DMA((nr, nq // 2)),
            pltpu.SemaphoreType.DMA((nr, nq // 2)),
        ],
        compiler_params=pltpu.CompilerParams(
            collective_id=0, has_side_effects=True, vmem_limit_bytes=VMEM_LIMIT
        ),
    )(block)


def spread_kernel(nr, nq, sides, pair, spread, strip, own_sem, send, recv, row_send, row_recv):
    r, q = lax.axis_index("row"), lax.axis_index("col")
    devices = nr * nq
    me = q * nr + r
    others = [lax.rem(me + d, devices) for d in range(1, devices)]
    places = [(lax.rem(other, nr), other // nr) for other in others]
    greet(places)
    copies = []
    for d in range(devices - 1):
        copies.append(
            pltpu.make_async_remote_copy(
                src_ref=sides.at[others[d]],
                dst_ref=spread.at[me],
                send_sem=send.at[d],
                recv_sem=recv.at[d],
                device_id=places[d],
                device_id_type=MESH,
            )
        )
        copies[-1].start()
    for e in range(1, nr):
        partner = lax.rem(r + e, nr)
        copies.append(
            pltpu.make_async_remote_copy(
                src_ref=pair.at[partner],
                dst_ref=strip.at[:, r],
                send_sem=row_send.at[e - 1],
                recv_sem=row_recv.at[e - 1],
                device_id=(partner, q),
                device_id_type=MESH,
            )
        )
        copies[-1].start()
    own = [
        pltpu.make_async_copy(sides.at[me], spread.at[me], own_sem.at[0]),
        pltpu.make_async_copy(pair.at[r], strip.at[:, r], own_sem.at[1]),
    ]
    for copy in own:
        copy.start()
    for copy in own:
        copy.wait()
    for copy in copies:
        copy.wait()


def spread_all(sides, pair, nr, nq):
    shape = (pair.shape[1], pair.shape[0]) + pair.shape[2:]
    return pl.pallas_call(
        functools.partial(spread_kernel, nr, nq),
        out_shape=[
            jax.ShapeDtypeStruct(sides.shape, sides.dtype),
            jax.ShapeDtypeStruct(shape, pair.dtype),
        ],
        in_specs=[pl.BlockSpec(memory_space=pltpu.VMEM)] * 2,
        out_specs=[pl.BlockSpec(memory_space=pltpu.VMEM)] * 2,
        scratch_shapes=[
            pltpu.SemaphoreType.DMA((2,)),
            pltpu.SemaphoreType.DMA((nr * nq - 1,)),
            pltpu.SemaphoreType.DMA((nr * nq - 1,)),
            pltpu.SemaphoreType.DMA((nr - 1,)),
            pltpu.SemaphoreType.DMA((nr - 1,)),
        ],
        compiler_params=pltpu.CompilerParams(
            collective_id=1, has_side_effects=True, vmem_limit_bytes=VMEM_LIMIT
        ),
    )(sides, pair)


def cut_spec(shape, dim, steps):
    block = tuple(n // steps if d == dim else n for d, n in enumerate(shape))
    return pl.BlockSpec(block, lambda c: tuple(c if d == dim else 0 for d in range(len(shape))))


def step_call(kernel, steps, ins, outs):
    return pl.pallas_call(
        kernel,
        grid=(steps,),
        in_specs=[cut_spec(a.shape, dim, steps) for a, dim in ins],
        out_specs=[cut_spec(shape, dim, steps) for shape, _, dim in outs],
        out_shape=[jax.ShapeDtypeStruct(shape, t) for shape, t, _ in outs],
        compiler_params=pltpu.CompilerParams(vmem_limit_bytes=VMEM_LIMIT),
    )(*[a for a, _ in ins])


def attend_and_return(ins, nr):
    columns, residues, channels = ins[0][0].shape
    block = (residues // nr, channels)
    return pl.pallas_call(
        functools.partial(attention_kernel, nr, columns),
        grid=(columns,),
        in_specs=[cut_spec(a.shape, dim, columns) for a, dim in ins],
        out_specs=pl.BlockSpec(memory_space=pl.ANY),
        out_shape=jax.ShapeDtypeStruct((nr, columns) + block, BF16),
        scratch_shapes=[
            pltpu.VMEM((columns, nr) + block, BF16),
            pltpu.SemaphoreType.DMA((columns,)),
            pltpu.SemaphoreType.DMA((nr - 1, columns)),
            pltpu.SemaphoreType.DMA((nr - 1, columns)),
        ],
        compiler_params=pltpu.CompilerParams(
            collective_id=2, has_side_effects=True, vmem_limit_bytes=VMEM_LIMIT
        ),
    )(*[a for a, _ in ins])


def on_device(
    pair,
    block_chain,
    block_valid,
    tri_norm_gain,
    tri_norm_bias,
    tri_in_weight,
    tri_gate_weight,
    out_norm_gain,
    out_norm_bias,
    tri_out_weight,
    att_norm_gain,
    att_norm_bias,
    qkvg_weight,
    bias_weight,
    inter_chain,
    att_out_weight,
):
    row_count, col_count, channels = pair.shape
    hidden = tri_out_weight.shape[0]
    row_devices = lax.axis_size("row")
    col_devices = lax.axis_size("col")
    devices = row_devices * col_devices
    residues = row_count * row_devices
    strip = col_count // row_devices
    axes = ("col", "row")
    residue_valid = jnp.repeat(block_valid, MB).astype(F32)
    residue_chain = jnp.repeat(block_chain, MB)
    strip_start = lax.axis_index("col") * col_count + lax.axis_index("row") * strip
    valid_j = lax.dynamic_slice_in_dim(residue_valid, strip_start, strip)[:, None]

    share = hidden // devices
    flat = strip * residues
    steps = strip // 2 if strip % 2 == 0 else 1
    by_column = jnp.swapaxes(pair, 0, 1)
    in_t = (
        tri_in_weight.reshape(channels, 2, 2, devices, share)
        .transpose(2, 3, 1, 4, 0)
        .reshape(4 * hidden, channels)
    )
    valid_rows = lax.dynamic_slice_in_dim(
        residue_valid, lax.axis_index("row") * row_count, row_count
    )
    valid_cols = lax.dynamic_slice_in_dim(
        residue_valid, lax.axis_index("col") * col_count, col_count
    )
    mask = (valid_cols[:, None] * valid_rows[None, :]).reshape(1, flat)
    (sides,) = step_call(
        project_kernel,
        steps,
        [
            (by_column, 0),
            (mask, 1),
            (tri_norm_gain[None, :], None),
            (tri_norm_bias[None, :], None),
            (in_t, None),
        ],
        [((2 * hidden, flat), BF16, 1)],
    )
    spread, own = spread_all(
        sides.reshape(devices, 2 * share, flat),
        by_column.reshape(row_devices, strip, row_count, channels),
        row_devices,
        col_devices,
    )
    own = own.reshape(strip, residues, channels)
    (tri_gate,) = step_call(
        gate_kernel,
        steps,
        [
            (own, 0),
            (tri_norm_gain[None, :], None),
            (tri_norm_bias[None, :], None),
            (tri_gate_weight, None),
        ],
        [((strip, residues, channels), F32, 0)],
    )
    spread = (
        spread.reshape(col_devices, row_devices, 2, share, col_count, row_count)
        .transpose(2, 3, 0, 4, 1, 5)
        .reshape(2, share, residues, residues)
    )
    product = jnp.einsum(
        "cki,ckj->cji", spread[0], spread[1], preferred_element_type=F32
    ).astype(BF16)
    product = jnp.swapaxes(product.reshape(share, devices, flat), 0, 1)
    product = lax.all_to_all(product, axes, split_axis=0, concat_axis=0, tiled=True)
    mid, bias = step_call(
        middle_kernel,
        steps,
        [
            (own, 0),
            (product.reshape(hidden, flat), 1),
            (tri_gate, 0),
            (out_norm_gain[:, None], None),
            (out_norm_bias[:, None], None),
            (tri_out_weight, None),
            (att_norm_gain[None, :], None),
            (att_norm_bias[None, :], None),
            (bias_weight.T, None),
        ],
        [((strip, residues, channels), BF16, 0), ((strip, H, residues), BF16, 0)],
    )
    bias = gather_all(bias, row_devices, col_devices).reshape(residues, H, residues)
    crossing = (residue_chain[:, None] != residue_chain[None, :]).astype(F32)
    extra = (
        jnp.swapaxes(bias, 0, 1).astype(F32)
        + inter_chain[:, None, None] * crossing[None]
        + (MASK_NEG * (residue_valid - 1.0))[None, None, :]
    )
    extra = jnp.pad(extra, ((0, 0), (0, 0), (0, -residues % 128)), constant_values=FILLED)
    result = attend_and_return(
        [
            (mid, 0),
            (extra, None),
            (residue_valid[:, None], None),
            (valid_j[:, :, None], 0),
            (att_norm_gain[None, :], None),
            (att_norm_bias[None, :], None),
            (qkvg_weight, None),
            (att_out_weight, None),
        ],
        row_devices,
    ).reshape(col_count, row_count, channels)
    return jnp.swapaxes(result, 0, 1)


def solution(mesh):
    placed = (P("row", "col", None),) + (P(),) * 15
    return jax.shard_map(
        on_device, mesh=mesh, in_specs=placed, out_specs=P("row", "col", None), check_vma=False
    )
```

```python
import functools

import jax
import jax.numpy as jnp
from jax import lax
from jax.experimental import pallas as pl
from jax.experimental.pallas import tpu as pltpu
from jax.sharding import PartitionSpec as P

H = 4
DH = 32
MB = 64

MASK_NEG = 10000.0
EPS = 1e-05
FILLED = -1e30
F32 = jnp.float32
BF16 = jnp.bfloat16
MESH = pl.DeviceIdType.MESH
VMEM_LIMIT = 48 * 1024 * 1024


def layer_norm(values, gain, shift, axis=-1):
    middle = jnp.mean(values, axis=axis, keepdims=True)
    centred = values - middle
    spread = jnp.mean(centred * centred, axis=axis, keepdims=True)
    return centred * lax.rsqrt(spread + EPS) * gain + shift


def dot_nt(left, right):
    return lax.dot_general(left, right, (((1,), (1,)), ((), ())), preferred_element_type=F32)


def dot_tn(left, right):
    return lax.dot_general(left, right, (((0,), (0,)), ((), ())), preferred_element_type=F32)


def dot_nn(left, right):
    return lax.dot_general(left, right, (((1,), (0,)), ((), ())), preferred_element_type=F32)


def project_kernel(pair_ref, mask_ref, gain_ref, shift_ref, in_t_ref, sides_ref):
    columns, rows, channels = pair_ref.shape
    flat = pair_ref[...].reshape(columns * rows, channels).astype(F32)
    normed = layer_norm(flat, gain_ref[...], shift_ref[...]).astype(BF16)
    proj = dot_nt(in_t_ref[...], normed)
    half = sides_ref.shape[0]
    sides_ref[...] = (mask_ref[...] * jax.nn.sigmoid(proj[:half]) * proj[half:]).astype(BF16)


def gate_kernel(pair_ref, gain_ref, shift_ref, gate_w_ref, gate_ref):
    columns, rows, channels = pair_ref.shape
    flat = pair_ref[...].reshape(columns * rows, channels).astype(F32)
    normed = layer_norm(flat, gain_ref[...], shift_ref[...]).astype(BF16)
    gate = jax.nn.sigmoid(dot_nn(normed, gate_w_ref[...]))
    gate_ref[...] = gate.reshape(columns, rows, channels)


def product_kernel(spread_ref, product_ref, ordered):
    step = pl.program_id(0)
    nr, sides, flat = spread_ref.shape
    share, residues = product_ref.shape[:2]
    rows = residues // nr
    count = flat // rows
    parts = [spread_ref[r].astype(F32) for r in range(nr)]
    lines = [
        jnp.concatenate([part[:, k * rows : (k + 1) * rows] for part in parts], axis=1)
        for k in range(count)
    ]
    block = jnp.swapaxes(jnp.stack(lines, axis=0), 0, 1)
    ordered[:, pl.ds(pl.multiple_of(step * count, 8), count), :] = block

    @pl.when(step == residues // count - 1)
    def _():
        for channel in range(share):
            left, right = ordered[channel].astype(BF16), ordered[share + channel].astype(BF16)
            product_ref[channel] = dot_tn(right, left).astype(BF16)


def middle_kernel(
    pair_ref,
    product_ref,
    gate_ref,
    out_gain_ref,
    out_shift_ref,
    out_w_ref,
    att_gain_ref,
    att_shift_ref,
    bias_t_ref,
    mid_ref,
    bias_ref,
):
    columns, rows, channels = pair_ref.shape
    normed = layer_norm(
        product_ref[...].astype(F32), out_gain_ref[...], out_shift_ref[...], axis=0
    ).astype(BF16)
    update = dot_tn(normed, out_w_ref[...])
    flat = pair_ref[...].reshape(columns * rows, channels).astype(F32)
    mid = (flat + gate_ref[...].reshape(columns * rows, channels) * update).astype(BF16)
    mid_ref[...] = mid.reshape(columns, rows, channels)
    att = layer_norm(mid.astype(F32), att_gain_ref[...], att_shift_ref[...]).astype(BF16)
    bias = dot_nt(bias_t_ref[...], att).astype(BF16)
    for column in range(columns):
        bias_ref[column] = bias[:, column * rows : (column + 1) * rows]


def stack_rows(parts):
    return jnp.concatenate([part for part in parts if part.shape[0]], axis=0)


def attention_kernel(
    nr,
    columns,
    mid_ref,
    extra_ref,
    valid_i_ref,
    valid_j_ref,
    gain_ref,
    shift_ref,
    qkvg_ref,
    out_w_ref,
    out,
    result,
    own_sem,
    send,
    recv,
):
    column = pl.program_id(0)
    r, q = lax.axis_index("row"), lax.axis_index("col")
    peers = [(lax.rem(r + e, nr), q) for e in range(1, nr)]
    barrier = pltpu.get_barrier_semaphore()

    def copies(c):
        return [
            pltpu.make_async_remote_copy(
                src_ref=result.at[c, peer[0]],
                dst_ref=out.at[r, c],
                send_sem=send.at[e, c],
                recv_sem=recv.at[e, c],
                device_id=peer,
                device_id_type=MESH,
            )
            for e, peer in enumerate(peers)
        ] + [pltpu.make_async_copy(result.at[c, r], out.at[r, c], own_sem.at[c])]

    @pl.when(column == 0)
    def _():
        for peer in peers:
            pl.semaphore_signal(barrier, inc=1, device_id=peer, device_id_type=MESH)

    width = H * DH
    mid = mid_ref[0].astype(F32)
    att = layer_norm(mid, gain_ref[...], shift_ref[...]).astype(BF16)
    heads = dot_nn(att, qkvg_ref[...])
    queries = (heads[:, :width] * DH ** (-0.5)).astype(BF16)
    keys = heads[:, width : 2 * width].astype(BF16)
    vals = heads[:, 2 * width : 3 * width].astype(BF16)
    gate = jax.nn.sigmoid(heads[:, 3 * width :])
    rows, padded = extra_ref.shape[1:]
    lane_head = lax.broadcasted_iota(jnp.int32, (rows, width), 1) // DH
    filler = jnp.zeros((padded - rows, width), BF16)
    key_rows, val_rows, one_rows = [], [], []
    for head in range(H):
        inside = (lane_head == head).astype(F32).astype(BF16)
        key_rows += [keys * inside, filler]
        val_rows += [vals * inside, filler]
        one_rows += [inside, filler]
    scores = dot_nt(queries, stack_rows(key_rows))
    powers = []
    for head in range(H):
        part = scores[:, head * padded : (head + 1) * padded] + extra_ref[head]
        powers.append(jnp.exp(part - jnp.max(part, axis=1, keepdims=True)).astype(BF16))
    sums = dot_nn(
        jnp.concatenate(powers, axis=1),
        jnp.concatenate([stack_rows(val_rows), stack_rows(one_rows)], axis=1),
    )
    gated = (gate * sums[:, :width] / sums[:, width:]).astype(BF16)
    update = dot_nn(gated, out_w_ref[...])
    mask = valid_i_ref[...] * valid_j_ref[0]
    rows = mid.shape[0] // nr
    result[column] = (mid + mask * update).astype(BF16).reshape(nr, rows, mid.shape[1])

    @pl.when(column == 0)
    def _():
        pl.semaphore_wait(barrier, len(peers))

    for copy in copies(column):
        copy.start()

    @pl.when(column == columns - 1)
    def _():
        for c in range(columns):
            for copy in copies(c):
                copy.wait()


def greet(peers):
    barrier = pltpu.get_barrier_semaphore()
    for peer in peers:
        pl.semaphore_signal(barrier, inc=1, device_id=peer, device_id_type=MESH)
    pl.semaphore_wait(barrier, len(peers))


def gather_kernel(
    nr, nq, src, out, own_sem, col_send, col_recv, row_send, row_recv, mate_send, mate_recv
):
    r, q = lax.axis_index("row"), lax.axis_index("col")
    row_peers = [(lax.rem(r + e, nr), q) for e in range(1, nr)]
    col_peers = [(r, lax.rem(q + 2 * d, nq)) for d in range(1, nq // 2)]
    mate = (r, q + 1 - 2 * lax.rem(q, 2))
    greet(row_peers + col_peers + [mate])

    def send(block, place, send_sem, recv_sem, peer):
        copy = pltpu.make_async_remote_copy(
            src_ref=block,
            dst_ref=out.at[place[0], place[1]],
            send_sem=send_sem,
            recv_sem=recv_sem,
            device_id=peer,
            device_id_type=MESH,
        )
        copy.start()
        return copy

    over_col = [
        send(src, (q, r), col_send.at[d], col_recv.at[d], peer) for d, peer in enumerate(col_peers)
    ]
    own = pltpu.make_async_copy(src, out.at[q, r], own_sem)
    own.start()
    over_row, to_mate = [], []
    for d in range(nq // 2):
        source = lax.rem(q + nq - 2 * d, nq)
        block = src if d == 0 else out.at[source, r]
        if d > 0:
            over_col[d - 1].wait_recv()
        over_row.append(
            [
                send(block, (source, r), row_send.at[e, d], row_recv.at[e, d], peer)
                for e, peer in enumerate(row_peers)
            ]
        )
        to_mate.append(send(block, (source, r), mate_send.at[0, d], mate_recv.at[0, d], mate))
    for d in range(nq // 2):
        source = lax.rem(q + nq - 2 * d, nq)
        for e in range(nr - 1):
            over_row[d][e].wait_recv()
            place = (source, lax.rem(r + nr - 1 - e, nr))
            to_mate.append(
                send(
                    out.at[place[0], place[1]],
                    place,
                    mate_send.at[e + 1, d],
                    mate_recv.at[e + 1, d],
                    mate,
                )
            )
    own.wait()
    for copy in to_mate:
        copy.wait()
    for copy in over_col + sum(over_row, []):
        copy.wait_send()


def gather_all(block, nr, nq):
    return pl.pallas_call(
        functools.partial(gather_kernel, nr, nq),
        out_shape=jax.ShapeDtypeStruct((nq, nr) + block.shape, block.dtype),
        in_specs=[pl.BlockSpec(memory_space=pltpu.VMEM)],
        out_specs=pl.BlockSpec(memory_space=pltpu.VMEM),
        scratch_shapes=[
            pltpu.SemaphoreType.DMA,
            pltpu.SemaphoreType.DMA((nq // 2 - 1,)),
            pltpu.SemaphoreType.DMA((nq // 2 - 1,)),
            pltpu.SemaphoreType.DMA((nr - 1, nq // 2)),
            pltpu.SemaphoreType.DMA((nr - 1, nq // 2)),
            pltpu.SemaphoreType.DMA((nr, nq // 2)),
            pltpu.SemaphoreType.DMA((nr, nq // 2)),
        ],
        compiler_params=pltpu.CompilerParams(
            collective_id=0, has_side_effects=True, vmem_limit_bytes=VMEM_LIMIT
        ),
    )(block)


def spread_kernel(nr, nq, sides, pair, spread, strip, own_sem, send, recv, row_send, row_recv):
    r, q = lax.axis_index("row"), lax.axis_index("col")
    devices = nr * nq
    me = q * nr + r
    others = [lax.rem(me + d, devices) for d in range(1, devices)]
    places = [(lax.rem(other, nr), other // nr) for other in others]
    greet(places)
    copies = []
    for d in range(devices - 1):
        copies.append(
            pltpu.make_async_remote_copy(
                src_ref=sides.at[others[d]],
                dst_ref=spread.at[me],
                send_sem=send.at[d],
                recv_sem=recv.at[d],
                device_id=places[d],
                device_id_type=MESH,
            )
        )
        copies[-1].start()
    for e in range(1, nr):
        partner = lax.rem(r + e, nr)
        copies.append(
            pltpu.make_async_remote_copy(
                src_ref=pair.at[partner],
                dst_ref=strip.at[:, r],
                send_sem=row_send.at[e - 1],
                recv_sem=row_recv.at[e - 1],
                device_id=(partner, q),
                device_id_type=MESH,
            )
        )
        copies[-1].start()
    own = [
        pltpu.make_async_copy(sides.at[me], spread.at[me], own_sem.at[0]),
        pltpu.make_async_copy(pair.at[r], strip.at[:, r], own_sem.at[1]),
    ]
    for copy in own:
        copy.start()
    for copy in own:
        copy.wait()
    for copy in copies:
        copy.wait()


def spread_all(sides, pair, nr, nq):
    shape = (pair.shape[1], pair.shape[0]) + pair.shape[2:]
    return pl.pallas_call(
        functools.partial(spread_kernel, nr, nq),
        out_shape=[
            jax.ShapeDtypeStruct(sides.shape, sides.dtype),
            jax.ShapeDtypeStruct(shape, pair.dtype),
        ],
        in_specs=[pl.BlockSpec(memory_space=pltpu.VMEM)] * 2,
        out_specs=[pl.BlockSpec(memory_space=pltpu.VMEM)] * 2,
        scratch_shapes=[
            pltpu.SemaphoreType.DMA((2,)),
            pltpu.SemaphoreType.DMA((nr * nq - 1,)),
            pltpu.SemaphoreType.DMA((nr * nq - 1,)),
            pltpu.SemaphoreType.DMA((nr - 1,)),
            pltpu.SemaphoreType.DMA((nr - 1,)),
        ],
        compiler_params=pltpu.CompilerParams(
            collective_id=1, has_side_effects=True, vmem_limit_bytes=VMEM_LIMIT
        ),
    )(sides, pair)


def cut_spec(shape, dim, steps):
    block = tuple(n // steps if d == dim else n for d, n in enumerate(shape))
    return pl.BlockSpec(block, lambda c: tuple(c if d == dim else 0 for d in range(len(shape))))


def step_call(kernel, steps, ins, outs):
    return pl.pallas_call(
        kernel,
        grid=(steps,),
        in_specs=[cut_spec(a.shape, dim, steps) for a, dim in ins],
        out_specs=[cut_spec(shape, dim, steps) for shape, _, dim in outs],
        out_shape=[jax.ShapeDtypeStruct(shape, t) for shape, t, _ in outs],
        compiler_params=pltpu.CompilerParams(vmem_limit_bytes=VMEM_LIMIT),
    )(*[a for a, _ in ins])


def attend_and_return(ins, nr):
    columns, residues, channels = ins[0][0].shape
    block = (residues // nr, channels)
    return pl.pallas_call(
        functools.partial(attention_kernel, nr, columns),
        grid=(columns,),
        in_specs=[cut_spec(a.shape, dim, columns) for a, dim in ins],
        out_specs=pl.BlockSpec(memory_space=pl.ANY),
        out_shape=jax.ShapeDtypeStruct((nr, columns) + block, BF16),
        scratch_shapes=[
            pltpu.VMEM((columns, nr) + block, BF16),
            pltpu.SemaphoreType.DMA((columns,)),
            pltpu.SemaphoreType.DMA((nr - 1, columns)),
            pltpu.SemaphoreType.DMA((nr - 1, columns)),
        ],
        compiler_params=pltpu.CompilerParams(
            collective_id=2, has_side_effects=True, vmem_limit_bytes=VMEM_LIMIT
        ),
    )(*[a for a, _ in ins])


def on_device(
    pair,
    block_chain,
    block_valid,
    tri_norm_gain,
    tri_norm_bias,
    tri_in_weight,
    tri_gate_weight,
    out_norm_gain,
    out_norm_bias,
    tri_out_weight,
    att_norm_gain,
    att_norm_bias,
    qkvg_weight,
    bias_weight,
    inter_chain,
    att_out_weight,
):
    row_count, col_count, channels = pair.shape
    hidden = tri_out_weight.shape[0]
    row_devices = lax.axis_size("row")
    col_devices = lax.axis_size("col")
    devices = row_devices * col_devices
    residues = row_count * row_devices
    strip = col_count // row_devices
    axes = ("col", "row")
    residue_valid = jnp.repeat(block_valid, MB).astype(F32)
    residue_chain = jnp.repeat(block_chain, MB)
    strip_start = lax.axis_index("col") * col_count + lax.axis_index("row") * strip
    valid_j = lax.dynamic_slice_in_dim(residue_valid, strip_start, strip)[:, None]

    share = hidden // devices
    flat = strip * residues
    steps = strip // 2 if strip % 2 == 0 else 1
    by_column = jnp.swapaxes(pair, 0, 1)
    in_t = (
        tri_in_weight.reshape(channels, 2, 2, devices, share)
        .transpose(2, 3, 1, 4, 0)
        .reshape(4 * hidden, channels)
    )
    valid_rows = lax.dynamic_slice_in_dim(
        residue_valid, lax.axis_index("row") * row_count, row_count
    )
    valid_cols = lax.dynamic_slice_in_dim(
        residue_valid, lax.axis_index("col") * col_count, col_count
    )
    mask = (valid_cols[:, None] * valid_rows[None, :]).reshape(1, flat)
    (sides,) = step_call(
        project_kernel,
        steps,
        [
            (by_column, 0),
            (mask, 1),
            (tri_norm_gain[None, :], None),
            (tri_norm_bias[None, :], None),
            (in_t, None),
        ],
        [((2 * hidden, flat), BF16, 1)],
    )
    spread, own = spread_all(
        sides.reshape(devices, 2 * share, flat),
        by_column.reshape(row_devices, strip, row_count, channels),
        row_devices,
        col_devices,
    )
    own = own.reshape(strip, residues, channels)
    (tri_gate,) = step_call(
        gate_kernel,
        steps,
        [
            (own, 0),
            (tri_norm_gain[None, :], None),
            (tri_norm_bias[None, :], None),
            (tri_gate_weight, None),
        ],
        [((strip, residues, channels), F32, 0)],
    )
    product = pl.pallas_call(
        product_kernel,
        grid=(col_devices,),
        in_specs=[cut_spec(spread.shape, 0, col_devices)],
        out_specs=cut_spec((share, residues, residues), None, col_devices),
        out_shape=jax.ShapeDtypeStruct((share, residues, residues), BF16),
        scratch_shapes=[pltpu.VMEM((2 * share, residues, residues), F32)],
        compiler_params=pltpu.CompilerParams(vmem_limit_bytes=VMEM_LIMIT),
    )(spread)
    product = jnp.swapaxes(product.reshape(share, devices, flat), 0, 1)
    product = lax.all_to_all(product, axes, split_axis=0, concat_axis=0, tiled=True)
    mid, bias = step_call(
        middle_kernel,
        steps,
        [
            (own, 0),
            (product.reshape(hidden, flat), 1),
            (tri_gate, 0),
            (out_norm_gain[:, None], None),
            (out_norm_bias[:, None], None),
            (tri_out_weight, None),
            (att_norm_gain[None, :], None),
            (att_norm_bias[None, :], None),
            (bias_weight.T, None),
        ],
        [((strip, residues, channels), BF16, 0), ((strip, H, residues), BF16, 0)],
    )
    bias = gather_all(bias, row_devices, col_devices).reshape(residues, H, residues)
    crossing = (residue_chain[:, None] != residue_chain[None, :]).astype(F32)
    extra = (
        jnp.swapaxes(bias, 0, 1).astype(F32)
        + inter_chain[:, None, None] * crossing[None]
        + (MASK_NEG * (residue_valid - 1.0))[None, None, :]
    )
    extra = jnp.pad(extra, ((0, 0), (0, 0), (0, -residues % 128)), constant_values=FILLED)
    result = attend_and_return(
        [
            (mid, 0),
            (extra, None),
            (residue_valid[:, None], None),
            (valid_j[:, :, None], 0),
            (att_norm_gain[None, :], None),
            (att_norm_bias[None, :], None),
            (qkvg_weight, None),
            (att_out_weight, None),
        ],
        row_devices,
    ).reshape(col_count, row_count, channels)
    return jnp.swapaxes(result, 0, 1)


def solution(mesh):
    placed = (P("row", "col", None),) + (P(),) * 15
    return jax.shard_map(
        on_device, mesh=mesh, in_specs=placed, out_specs=P("row", "col", None), check_vma=False
    )
```

```python
import functools

import jax
import jax.numpy as jnp
from jax import lax
from jax.experimental import pallas as pl
from jax.experimental.pallas import tpu as pltpu
from jax.sharding import PartitionSpec as P

H = 4
DH = 32
MB = 64

MASK_NEG = 10000.0
EPS = 1e-05
FILLED = -1e30
F32 = jnp.float32
BF16 = jnp.bfloat16
MESH = pl.DeviceIdType.MESH
VMEM_LIMIT = 48 * 1024 * 1024


def layer_norm(values, gain, shift, axis=-1):
    middle = jnp.mean(values, axis=axis, keepdims=True)
    centred = values - middle
    spread = jnp.mean(centred * centred, axis=axis, keepdims=True)
    return centred * lax.rsqrt(spread + EPS) * gain + shift


def dot_nt(left, right):
    return lax.dot_general(left, right, (((1,), (1,)), ((), ())), preferred_element_type=F32)


def dot_tn(left, right):
    return lax.dot_general(left, right, (((0,), (0,)), ((), ())), preferred_element_type=F32)


def dot_nn(left, right):
    return lax.dot_general(left, right, (((1,), (0,)), ((), ())), preferred_element_type=F32)


def project_kernel(pair_ref, mask_ref, gain_ref, shift_ref, in_t_ref, sides_ref):
    columns, rows, channels = pair_ref.shape
    flat = pair_ref[...].reshape(columns * rows, channels).astype(F32)
    normed = layer_norm(flat, gain_ref[...], shift_ref[...]).astype(BF16)
    proj = dot_nt(in_t_ref[...], normed)
    half = sides_ref.shape[0]
    sides_ref[...] = (mask_ref[...] * jax.nn.sigmoid(proj[:half]) * proj[half:]).astype(BF16)


def gate_kernel(pair_ref, gain_ref, shift_ref, gate_w_ref, gate_ref):
    columns, rows, channels = pair_ref.shape
    flat = pair_ref[...].reshape(columns * rows, channels).astype(F32)
    normed = layer_norm(flat, gain_ref[...], shift_ref[...]).astype(BF16)
    gate = jax.nn.sigmoid(dot_nn(normed, gate_w_ref[...]))
    gate_ref[...] = gate.reshape(columns, rows, channels)


def product_kernel(spread_ref, product_ref, ordered):
    step = pl.program_id(0)
    nr, sides, flat = spread_ref.shape
    share, residues = product_ref.shape[:2]
    rows = residues // nr
    count = flat // rows
    parts = [spread_ref[r].astype(F32) for r in range(nr)]
    lines = [
        jnp.concatenate([part[:, k * rows : (k + 1) * rows] for part in parts], axis=1)
        for k in range(count)
    ]
    block = jnp.swapaxes(jnp.stack(lines, axis=0), 0, 1)
    ordered[:, pl.ds(pl.multiple_of(step * count, 8), count), :] = block

    @pl.when(step == residues // count - 1)
    def _():
        for channel in range(share):
            left, right = ordered[channel].astype(BF16), ordered[share + channel].astype(BF16)
            product_ref[channel] = dot_tn(right, left).astype(BF16)


def middle_kernel(
    pair_ref,
    product_ref,
    gate_ref,
    out_gain_ref,
    out_shift_ref,
    out_w_ref,
    att_gain_ref,
    att_shift_ref,
    bias_t_ref,
    mid_ref,
    bias_ref,
):
    columns, rows, channels = pair_ref.shape
    normed = layer_norm(
        product_ref[...].astype(F32), out_gain_ref[...], out_shift_ref[...], axis=0
    ).astype(BF16)
    update = dot_tn(normed, out_w_ref[...])
    flat = pair_ref[...].reshape(columns * rows, channels).astype(F32)
    mid = (flat + gate_ref[...].reshape(columns * rows, channels) * update).astype(BF16)
    mid_ref[...] = mid.reshape(columns, rows, channels)
    att = layer_norm(mid.astype(F32), att_gain_ref[...], att_shift_ref[...]).astype(BF16)
    bias = dot_nt(bias_t_ref[...], att).astype(BF16)
    for column in range(columns):
        bias_ref[column] = bias[:, column * rows : (column + 1) * rows]


def stack_rows(parts):
    return jnp.concatenate([part for part in parts if part.shape[0]], axis=0)


def attention_kernel(
    nr,
    columns,
    mid_ref,
    extra_ref,
    valid_i_ref,
    valid_j_ref,
    qkv_ref,
    gate_ref,
    out_w_ref,
    out,
    result,
    own_sem,
    send,
    recv,
):
    column = pl.program_id(0)
    r, q = lax.axis_index("row"), lax.axis_index("col")
    peers = [(lax.rem(r + e, nr), q) for e in range(1, nr)]
    barrier = pltpu.get_barrier_semaphore()

    def copies(c):
        return [
            pltpu.make_async_remote_copy(
                src_ref=result.at[c, peer[0]],
                dst_ref=out.at[r, c],
                send_sem=send.at[e, c],
                recv_sem=recv.at[e, c],
                device_id=peer,
                device_id_type=MESH,
            )
            for e, peer in enumerate(peers)
        ] + [pltpu.make_async_copy(result.at[c, r], out.at[r, c], own_sem.at[c])]

    @pl.when(column == 0)
    def _():
        for peer in peers:
            pl.semaphore_signal(barrier, inc=1, device_id=peer, device_id_type=MESH)

    width = H * DH
    mid = mid_ref[0].astype(F32)
    queries = qkv_ref[0, :, :width]
    keys = qkv_ref[0, :, width : 2 * width]
    vals = qkv_ref[0, :, 2 * width :]
    gate = gate_ref[0]
    rows, padded = extra_ref.shape[1:]
    lane_head = lax.broadcasted_iota(jnp.int32, (rows, width), 1) // DH
    filler = jnp.zeros((padded - rows, width), BF16)
    key_rows, val_rows, one_rows = [], [], []
    for head in range(H):
        inside = (lane_head == head).astype(F32).astype(BF16)
        key_rows += [keys * inside, filler]
        val_rows += [vals * inside, filler]
        one_rows += [inside, filler]
    scores = dot_nt(queries, stack_rows(key_rows))
    powers = []
    for head in range(H):
        part = scores[:, head * padded : (head + 1) * padded] + extra_ref[head]
        powers.append(jnp.exp(part - jnp.max(part, axis=1, keepdims=True)).astype(BF16))
    sums = dot_nn(
        jnp.concatenate(powers, axis=1),
        jnp.concatenate([stack_rows(val_rows), stack_rows(one_rows)], axis=1),
    )
    gated = (gate * sums[:, :width] / sums[:, width:]).astype(BF16)
    update = dot_nn(gated, out_w_ref[...])
    mask = valid_i_ref[...] * valid_j_ref[0]
    rows = mid.shape[0] // nr
    result[column] = (mid + mask * update).astype(BF16).reshape(nr, rows, mid.shape[1])

    @pl.when(column == 0)
    def _():
        pl.semaphore_wait(barrier, len(peers))

    for copy in copies(column):
        copy.start()

    @pl.when(column == columns - 1)
    def _():
        for c in range(columns):
            for copy in copies(c):
                copy.wait()


def greet(peers):
    barrier = pltpu.get_barrier_semaphore()
    for peer in peers:
        pl.semaphore_signal(barrier, inc=1, device_id=peer, device_id_type=MESH)
    pl.semaphore_wait(barrier, len(peers))


def gather_kernel(
    nr,
    nq,
    src,
    mid_ref,
    gain_ref,
    shift_ref,
    qkvg_ref,
    out,
    qkv_ref,
    gate_ref,
    own_sem,
    col_send,
    col_recv,
    row_send,
    row_recv,
    mate_send,
    mate_recv,
):
    r, q = lax.axis_index("row"), lax.axis_index("col")
    row_peers = [(lax.rem(r + e, nr), q) for e in range(1, nr)]
    col_peers = [(r, lax.rem(q + 2 * d, nq)) for d in range(1, nq // 2)]
    mate = (r, q + 1 - 2 * lax.rem(q, 2))
    greet(row_peers + col_peers + [mate])

    def send(block, place, send_sem, recv_sem, peer):
        copy = pltpu.make_async_remote_copy(
            src_ref=block,
            dst_ref=out.at[place[0], place[1]],
            send_sem=send_sem,
            recv_sem=recv_sem,
            device_id=peer,
            device_id_type=MESH,
        )
        copy.start()
        return copy

    over_col = [
        send(src, (q, r), col_send.at[d], col_recv.at[d], peer) for d, peer in enumerate(col_peers)
    ]
    own = pltpu.make_async_copy(src, out.at[q, r], own_sem)
    own.start()
    over_row, to_mate = [], []
    width = H * DH
    columns = mid_ref.shape[0]

    def project(column, carry):
        att = layer_norm(mid_ref[column].astype(F32), gain_ref[...], shift_ref[...]).astype(BF16)
        heads = dot_nn(att, qkvg_ref[...])
        qkv_ref[column, :, :width] = (heads[:, :width] * DH ** (-0.5)).astype(BF16)
        qkv_ref[column, :, width:] = heads[:, width : 3 * width].astype(BF16)
        gate_ref[column] = jax.nn.sigmoid(heads[:, 3 * width :])
        return carry

    for d in range(nq // 2):
        if d == 1:
            lax.fori_loop(0, columns // 2, project, 0)
        source = lax.rem(q + nq - 2 * d, nq)
        block = src if d == 0 else out.at[source, r]
        if d > 0:
            over_col[d - 1].wait_recv()
        over_row.append(
            [
                send(block, (source, r), row_send.at[e, d], row_recv.at[e, d], peer)
                for e, peer in enumerate(row_peers)
            ]
        )
        to_mate.append(send(block, (source, r), mate_send.at[0, d], mate_recv.at[0, d], mate))
    lax.fori_loop(columns // 2, columns, project, 0)
    for d in range(nq // 2):
        source = lax.rem(q + nq - 2 * d, nq)
        for e in range(nr - 1):
            over_row[d][e].wait_recv()
            place = (source, lax.rem(r + nr - 1 - e, nr))
            to_mate.append(
                send(
                    out.at[place[0], place[1]],
                    place,
                    mate_send.at[e + 1, d],
                    mate_recv.at[e + 1, d],
                    mate,
                )
            )
    own.wait()
    for copy in to_mate:
        copy.wait()
    for copy in over_col + sum(over_row, []):
        copy.wait_send()


def gather_all(block, mid, gain, shift, qkvg, nr, nq):
    width = H * DH
    return pl.pallas_call(
        functools.partial(gather_kernel, nr, nq),
        out_shape=[
            jax.ShapeDtypeStruct((nq, nr) + block.shape, block.dtype),
            jax.ShapeDtypeStruct(mid.shape[:2] + (3 * width,), BF16),
            jax.ShapeDtypeStruct(mid.shape[:2] + (width,), F32),
        ],
        in_specs=[pl.BlockSpec(memory_space=pltpu.VMEM)] * 5,
        out_specs=[pl.BlockSpec(memory_space=pltpu.VMEM)] * 3,
        scratch_shapes=[
            pltpu.SemaphoreType.DMA,
            pltpu.SemaphoreType.DMA((nq // 2 - 1,)),
            pltpu.SemaphoreType.DMA((nq // 2 - 1,)),
            pltpu.SemaphoreType.DMA((nr - 1, nq // 2)),
            pltpu.SemaphoreType.DMA((nr - 1, nq // 2)),
            pltpu.SemaphoreType.DMA((nr, nq // 2)),
            pltpu.SemaphoreType.DMA((nr, nq // 2)),
        ],
        compiler_params=pltpu.CompilerParams(
            collective_id=0, has_side_effects=True, vmem_limit_bytes=VMEM_LIMIT
        ),
    )(block, mid, gain, shift, qkvg)


def spread_kernel(nr, nq, sides, pair, spread, strip, own_sem, send, recv, row_send, row_recv):
    r, q = lax.axis_index("row"), lax.axis_index("col")
    devices = nr * nq
    me = q * nr + r
    others = [lax.rem(me + d, devices) for d in range(1, devices)]
    places = [(lax.rem(other, nr), other // nr) for other in others]
    greet(places)
    copies = []
    for d in range(devices - 1):
        copies.append(
            pltpu.make_async_remote_copy(
                src_ref=sides.at[others[d]],
                dst_ref=spread.at[me],
                send_sem=send.at[d],
                recv_sem=recv.at[d],
                device_id=places[d],
                device_id_type=MESH,
            )
        )
        copies[-1].start()
    for e in range(1, nr):
        partner = lax.rem(r + e, nr)
        copies.append(
            pltpu.make_async_remote_copy(
                src_ref=pair.at[partner],
                dst_ref=strip.at[:, r],
                send_sem=row_send.at[e - 1],
                recv_sem=row_recv.at[e - 1],
                device_id=(partner, q),
                device_id_type=MESH,
            )
        )
        copies[-1].start()
    own = [
        pltpu.make_async_copy(sides.at[me], spread.at[me], own_sem.at[0]),
        pltpu.make_async_copy(pair.at[r], strip.at[:, r], own_sem.at[1]),
    ]
    for copy in own:
        copy.start()
    for copy in own:
        copy.wait()
    for copy in copies:
        copy.wait()


def spread_all(sides, pair, nr, nq):
    shape = (pair.shape[1], pair.shape[0]) + pair.shape[2:]
    return pl.pallas_call(
        functools.partial(spread_kernel, nr, nq),
        out_shape=[
            jax.ShapeDtypeStruct(sides.shape, sides.dtype),
            jax.ShapeDtypeStruct(shape, pair.dtype),
        ],
        in_specs=[pl.BlockSpec(memory_space=pltpu.VMEM)] * 2,
        out_specs=[pl.BlockSpec(memory_space=pltpu.VMEM)] * 2,
        scratch_shapes=[
            pltpu.SemaphoreType.DMA((2,)),
            pltpu.SemaphoreType.DMA((nr * nq - 1,)),
            pltpu.SemaphoreType.DMA((nr * nq - 1,)),
            pltpu.SemaphoreType.DMA((nr - 1,)),
            pltpu.SemaphoreType.DMA((nr - 1,)),
        ],
        compiler_params=pltpu.CompilerParams(
            collective_id=1, has_side_effects=True, vmem_limit_bytes=VMEM_LIMIT
        ),
    )(sides, pair)


def cut_spec(shape, dim, steps):
    block = tuple(n // steps if d == dim else n for d, n in enumerate(shape))
    return pl.BlockSpec(block, lambda c: tuple(c if d == dim else 0 for d in range(len(shape))))


def step_call(kernel, steps, ins, outs):
    return pl.pallas_call(
        kernel,
        grid=(steps,),
        in_specs=[cut_spec(a.shape, dim, steps) for a, dim in ins],
        out_specs=[cut_spec(shape, dim, steps) for shape, _, dim in outs],
        out_shape=[jax.ShapeDtypeStruct(shape, t) for shape, t, _ in outs],
        compiler_params=pltpu.CompilerParams(vmem_limit_bytes=VMEM_LIMIT),
    )(*[a for a, _ in ins])


def attend_and_return(ins, nr):
    columns, residues, channels = ins[0][0].shape
    block = (residues // nr, channels)
    return pl.pallas_call(
        functools.partial(attention_kernel, nr, columns),
        grid=(columns,),
        in_specs=[cut_spec(a.shape, dim, columns) for a, dim in ins],
        out_specs=pl.BlockSpec(memory_space=pl.ANY),
        out_shape=jax.ShapeDtypeStruct((nr, columns) + block, BF16),
        scratch_shapes=[
            pltpu.VMEM((columns, nr) + block, BF16),
            pltpu.SemaphoreType.DMA((columns,)),
            pltpu.SemaphoreType.DMA((nr - 1, columns)),
            pltpu.SemaphoreType.DMA((nr - 1, columns)),
        ],
        compiler_params=pltpu.CompilerParams(
            collective_id=2, has_side_effects=True, vmem_limit_bytes=VMEM_LIMIT
        ),
    )(*[a for a, _ in ins])


def on_device(
    pair,
    block_chain,
    block_valid,
    tri_norm_gain,
    tri_norm_bias,
    tri_in_weight,
    tri_gate_weight,
    out_norm_gain,
    out_norm_bias,
    tri_out_weight,
    att_norm_gain,
    att_norm_bias,
    qkvg_weight,
    bias_weight,
    inter_chain,
    att_out_weight,
):
    row_count, col_count, channels = pair.shape
    hidden = tri_out_weight.shape[0]
    row_devices = lax.axis_size("row")
    col_devices = lax.axis_size("col")
    devices = row_devices * col_devices
    residues = row_count * row_devices
    strip = col_count // row_devices
    axes = ("col", "row")
    residue_valid = jnp.repeat(block_valid, MB).astype(F32)
    residue_chain = jnp.repeat(block_chain, MB)
    strip_start = lax.axis_index("col") * col_count + lax.axis_index("row") * strip
    valid_j = lax.dynamic_slice_in_dim(residue_valid, strip_start, strip)[:, None]

    share = hidden // devices
    flat = strip * residues
    steps = strip // 2 if strip % 2 == 0 else 1
    by_column = jnp.swapaxes(pair, 0, 1)
    in_t = (
        tri_in_weight.reshape(channels, 2, 2, devices, share)
        .transpose(2, 3, 1, 4, 0)
        .reshape(4 * hidden, channels)
    )
    valid_rows = lax.dynamic_slice_in_dim(
        residue_valid, lax.axis_index("row") * row_count, row_count
    )
    valid_cols = lax.dynamic_slice_in_dim(
        residue_valid, lax.axis_index("col") * col_count, col_count
    )
    mask = (valid_cols[:, None] * valid_rows[None, :]).reshape(1, flat)
    (sides,) = step_call(
        project_kernel,
        steps,
        [
            (by_column, 0),
            (mask, 1),
            (tri_norm_gain[None, :], None),
            (tri_norm_bias[None, :], None),
            (in_t, None),
        ],
        [((2 * hidden, flat), BF16, 1)],
    )
    spread, own = spread_all(
        sides.reshape(devices, 2 * share, flat),
        by_column.reshape(row_devices, strip, row_count, channels),
        row_devices,
        col_devices,
    )
    own = own.reshape(strip, residues, channels)
    (tri_gate,) = step_call(
        gate_kernel,
        steps,
        [
            (own, 0),
            (tri_norm_gain[None, :], None),
            (tri_norm_bias[None, :], None),
            (tri_gate_weight, None),
        ],
        [((strip, residues, channels), F32, 0)],
    )
    product = pl.pallas_call(
        product_kernel,
        grid=(col_devices,),
        in_specs=[cut_spec(spread.shape, 0, col_devices)],
        out_specs=cut_spec((share, residues, residues), None, col_devices),
        out_shape=jax.ShapeDtypeStruct((share, residues, residues), BF16),
        scratch_shapes=[pltpu.VMEM((2 * share, residues, residues), F32)],
        compiler_params=pltpu.CompilerParams(vmem_limit_bytes=VMEM_LIMIT),
    )(spread)
    product = jnp.swapaxes(product.reshape(share, devices, flat), 0, 1)
    product = lax.all_to_all(product, axes, split_axis=0, concat_axis=0, tiled=True)
    mid, bias = step_call(
        middle_kernel,
        steps,
        [
            (own, 0),
            (product.reshape(hidden, flat), 1),
            (tri_gate, 0),
            (out_norm_gain[:, None], None),
            (out_norm_bias[:, None], None),
            (tri_out_weight, None),
            (att_norm_gain[None, :], None),
            (att_norm_bias[None, :], None),
            (bias_weight.T, None),
        ],
        [((strip, residues, channels), BF16, 0), ((strip, H, residues), BF16, 0)],
    )
    bias, qkv, gate = gather_all(
        bias,
        mid,
        att_norm_gain[None, :],
        att_norm_bias[None, :],
        qkvg_weight,
        row_devices,
        col_devices,
    )
    bias = bias.reshape(residues, H, residues)
    crossing = (residue_chain[:, None] != residue_chain[None, :]).astype(F32)
    extra = (
        jnp.swapaxes(bias, 0, 1).astype(F32)
        + inter_chain[:, None, None] * crossing[None]
        + (MASK_NEG * (residue_valid - 1.0))[None, None, :]
    )
    extra = jnp.pad(extra, ((0, 0), (0, 0), (0, -residues % 128)), constant_values=FILLED)
    result = attend_and_return(
        [
            (mid, 0),
            (extra, None),
            (residue_valid[:, None], None),
            (valid_j[:, :, None], 0),
            (qkv, 0),
            (gate, 0),
            (att_out_weight, None),
        ],
        row_devices,
    ).reshape(col_count, row_count, channels)
    return jnp.swapaxes(result, 0, 1)


def solution(mesh):
    placed = (P("row", "col", None),) + (P(),) * 15
    return jax.shard_map(
        on_device, mesh=mesh, in_specs=placed, out_specs=P("row", "col", None), check_vma=False
    )
```

```python
import functools

import jax
import jax.numpy as jnp
from jax import lax
from jax.experimental import pallas as pl
from jax.experimental.pallas import tpu as pltpu
from jax.sharding import PartitionSpec as P

H = 4
DH = 32
MB = 64

MASK_NEG = 10000.0
EPS = 1e-05
FILLED = -1e30
F32 = jnp.float32
BF16 = jnp.bfloat16
MESH = pl.DeviceIdType.MESH
VMEM_LIMIT = 48 * 1024 * 1024


def layer_norm(values, gain, shift, axis=-1):
    middle = jnp.mean(values, axis=axis, keepdims=True)
    centred = values - middle
    spread = jnp.mean(centred * centred, axis=axis, keepdims=True)
    return centred * lax.rsqrt(spread + EPS) * gain + shift


def dot_nt(left, right):
    return lax.dot_general(left, right, (((1,), (1,)), ((), ())), preferred_element_type=F32)


def dot_tn(left, right):
    return lax.dot_general(left, right, (((0,), (0,)), ((), ())), preferred_element_type=F32)


def dot_nn(left, right):
    return lax.dot_general(left, right, (((1,), (0,)), ((), ())), preferred_element_type=F32)


def project_kernel(pair_ref, mask_ref, gain_ref, shift_ref, in_t_ref, sides_ref):
    columns, rows, channels = pair_ref.shape
    flat = pair_ref[...].reshape(columns * rows, channels).astype(F32)
    normed = layer_norm(flat, gain_ref[...], shift_ref[...]).astype(BF16)
    proj = dot_nt(in_t_ref[...], normed)
    half = sides_ref.shape[0]
    sides_ref[...] = (mask_ref[...] * jax.nn.sigmoid(proj[:half]) * proj[half:]).astype(BF16)


def gate_kernel(pair_ref, gain_ref, shift_ref, gate_w_ref, gate_ref):
    columns, rows, channels = pair_ref.shape
    flat = pair_ref[...].reshape(columns * rows, channels).astype(F32)
    normed = layer_norm(flat, gain_ref[...], shift_ref[...]).astype(BF16)
    gate = jax.nn.sigmoid(dot_nn(normed, gate_w_ref[...]))
    gate_ref[...] = gate.reshape(columns, rows, channels)


def product_kernel(spread_ref, product_ref, ordered):
    step = pl.program_id(0)
    nr, sides, flat = spread_ref.shape
    share, residues = product_ref.shape[:2]
    rows = residues // nr
    count = flat // rows
    parts = [spread_ref[r].astype(F32) for r in range(nr)]
    lines = [
        jnp.concatenate([part[:, k * rows : (k + 1) * rows] for part in parts], axis=1)
        for k in range(count)
    ]
    block = jnp.swapaxes(jnp.stack(lines, axis=0), 0, 1)
    ordered[:, pl.ds(pl.multiple_of(step * count, 8), count), :] = block

    @pl.when(step == residues // count - 1)
    def _():
        for channel in range(share):
            left, right = ordered[channel].astype(BF16), ordered[share + channel].astype(BF16)
            product_ref[channel] = dot_tn(right, left).astype(BF16)


def middle_kernel(
    pair_ref,
    product_ref,
    gate_ref,
    out_gain_ref,
    out_shift_ref,
    out_w_ref,
    att_gain_ref,
    att_shift_ref,
    bias_t_ref,
    mid_ref,
    bias_ref,
):
    columns, rows, channels = pair_ref.shape
    normed = layer_norm(
        product_ref[...].astype(F32), out_gain_ref[...], out_shift_ref[...], axis=0
    ).astype(BF16)
    update = dot_tn(normed, out_w_ref[...])
    flat = pair_ref[...].reshape(columns * rows, channels).astype(F32)
    mid = (flat + gate_ref[...].reshape(columns * rows, channels) * update).astype(BF16)
    mid_ref[...] = mid.reshape(columns, rows, channels)
    att = layer_norm(mid.astype(F32), att_gain_ref[...], att_shift_ref[...]).astype(BF16)
    bias = dot_nt(bias_t_ref[...], att).astype(BF16)
    for column in range(columns):
        bias_ref[column] = bias[:, column * rows : (column + 1) * rows]


def stack_rows(parts):
    return jnp.concatenate([part for part in parts if part.shape[0]], axis=0)


def attention_kernel(
    nr,
    columns,
    mid_ref,
    extra_ref,
    valid_i_ref,
    valid_j_ref,
    qkv_ref,
    gate_ref,
    out_w_ref,
    out,
    result,
    own_sem,
    send,
    recv,
):
    column = pl.program_id(0)
    r, q = lax.axis_index("row"), lax.axis_index("col")
    peers = [(lax.rem(r + e, nr), q) for e in range(1, nr)]
    barrier = pltpu.get_barrier_semaphore()

    def copies(c):
        return [
            pltpu.make_async_remote_copy(
                src_ref=result.at[c, peer[0]],
                dst_ref=out.at[r, c],
                send_sem=send.at[e, c],
                recv_sem=recv.at[e, c],
                device_id=peer,
                device_id_type=MESH,
            )
            for e, peer in enumerate(peers)
        ] + [pltpu.make_async_copy(result.at[c, r], out.at[r, c], own_sem.at[c])]

    @pl.when(column == 0)
    def _():
        for peer in peers:
            pl.semaphore_signal(barrier, inc=1, device_id=peer, device_id_type=MESH)

    width = H * DH
    mid = mid_ref[0].astype(F32)
    queries = qkv_ref[0, :, :width]
    keys = qkv_ref[0, :, width : 2 * width]
    vals = qkv_ref[0, :, 2 * width :]
    gate = gate_ref[0]
    rows, padded = extra_ref.shape[1:]
    lane_head = lax.broadcasted_iota(jnp.int32, (rows, width), 1) // DH
    filler = jnp.zeros((padded - rows, width), BF16)
    key_rows, val_rows, one_rows = [], [], []
    for head in range(H):
        inside = (lane_head == head).astype(F32).astype(BF16)
        key_rows += [keys * inside, filler]
        val_rows += [vals * inside, filler]
        one_rows += [inside, filler]
    scores = dot_nt(queries, stack_rows(key_rows))
    powers = []
    for head in range(H):
        part = scores[:, head * padded : (head + 1) * padded] + extra_ref[head]
        powers.append(jnp.exp(part - jnp.max(part, axis=1, keepdims=True)).astype(BF16))
    sums = dot_nn(
        jnp.concatenate(powers, axis=1),
        jnp.concatenate([stack_rows(val_rows), stack_rows(one_rows)], axis=1),
    )
    gated = (gate * sums[:, :width] / sums[:, width:]).astype(BF16)
    update = dot_nn(gated, out_w_ref[...])
    mask = valid_i_ref[...] * valid_j_ref[0]
    rows = mid.shape[0] // nr
    result[column] = (mid + mask * update).astype(BF16).reshape(nr, rows, mid.shape[1])

    @pl.when(column == 0)
    def _():
        pl.semaphore_wait(barrier, len(peers))

    for copy in copies(column):
        copy.start()

    @pl.when(column == columns - 1)
    def _():
        for c in range(columns):
            for copy in copies(c):
                copy.wait()


def greet(peers):
    barrier = pltpu.get_barrier_semaphore()
    for peer in peers:
        pl.semaphore_signal(barrier, inc=1, device_id=peer, device_id_type=MESH)
    pl.semaphore_wait(barrier, len(peers))


def gather_kernel(
    nr,
    nq,
    src,
    mid_ref,
    gain_ref,
    shift_ref,
    qkvg_ref,
    out,
    qkv_ref,
    gate_ref,
    own_sem,
    col_send,
    col_recv,
    row_send,
    row_recv,
    mate_send,
    mate_recv,
):
    r, q = lax.axis_index("row"), lax.axis_index("col")
    row_peers = [(lax.rem(r + e, nr), q) for e in range(1, nr)]
    col_peers = [(r, lax.rem(q + 2 * d, nq)) for d in range(1, nq // 2)]
    mate = (r, q + 1 - 2 * lax.rem(q, 2))
    greet(row_peers + col_peers + [mate])

    def send(block, place, send_sem, recv_sem, peer):
        copy = pltpu.make_async_remote_copy(
            src_ref=block,
            dst_ref=out.at[place[0], place[1]],
            send_sem=send_sem,
            recv_sem=recv_sem,
            device_id=peer,
            device_id_type=MESH,
        )
        copy.start()
        return copy

    over_col = [
        send(src, (q, r), col_send.at[d], col_recv.at[d], peer) for d, peer in enumerate(col_peers)
    ]
    own = pltpu.make_async_copy(src, out.at[q, r], own_sem)
    own.start()
    over_row, to_mate = [], []
    width = H * DH
    columns = mid_ref.shape[0]

    def project(column, carry):
        att = layer_norm(mid_ref[column].astype(F32), gain_ref[...], shift_ref[...]).astype(BF16)
        heads = dot_nn(att, qkvg_ref[...])
        qkv_ref[column, :, :width] = (heads[:, :width] * DH ** (-0.5)).astype(BF16)
        qkv_ref[column, :, width:] = heads[:, width : 3 * width].astype(BF16)
        gate_ref[column] = jax.nn.sigmoid(heads[:, 3 * width :])
        return carry

    for d in range(nq // 2):
        if d == 1:
            lax.fori_loop(0, columns // 5, project, 0)
        source = lax.rem(q + nq - 2 * d, nq)
        block = src if d == 0 else out.at[source, r]
        if d > 0:
            over_col[d - 1].wait_recv()
        over_row.append(
            [
                send(block, (source, r), row_send.at[e, d], row_recv.at[e, d], peer)
                for e, peer in enumerate(row_peers)
            ]
        )
        to_mate.append(send(block, (source, r), mate_send.at[0, d], mate_recv.at[0, d], mate))
    lax.fori_loop(columns // 5, columns, project, 0)
    for d in range(nq // 2):
        source = lax.rem(q + nq - 2 * d, nq)
        for e in range(nr - 1):
            over_row[d][e].wait_recv()
            place = (source, lax.rem(r + nr - 1 - e, nr))
            to_mate.append(
                send(
                    out.at[place[0], place[1]],
                    place,
                    mate_send.at[e + 1, d],
                    mate_recv.at[e + 1, d],
                    mate,
                )
            )
    own.wait()
    for copy in to_mate:
        copy.wait()
    for copy in over_col + sum(over_row, []):
        copy.wait_send()


def gather_all(block, mid, gain, shift, qkvg, nr, nq):
    width = H * DH
    return pl.pallas_call(
        functools.partial(gather_kernel, nr, nq),
        out_shape=[
            jax.ShapeDtypeStruct((nq, nr) + block.shape, block.dtype),
            jax.ShapeDtypeStruct(mid.shape[:2] + (3 * width,), BF16),
            jax.ShapeDtypeStruct(mid.shape[:2] + (width,), F32),
        ],
        in_specs=[pl.BlockSpec(memory_space=pltpu.VMEM)] * 5,
        out_specs=[pl.BlockSpec(memory_space=pltpu.VMEM)] * 3,
        scratch_shapes=[
            pltpu.SemaphoreType.DMA,
            pltpu.SemaphoreType.DMA((nq // 2 - 1,)),
            pltpu.SemaphoreType.DMA((nq // 2 - 1,)),
            pltpu.SemaphoreType.DMA((nr - 1, nq // 2)),
            pltpu.SemaphoreType.DMA((nr - 1, nq // 2)),
            pltpu.SemaphoreType.DMA((nr, nq // 2)),
            pltpu.SemaphoreType.DMA((nr, nq // 2)),
        ],
        compiler_params=pltpu.CompilerParams(
            collective_id=0, has_side_effects=True, vmem_limit_bytes=VMEM_LIMIT
        ),
    )(block, mid, gain, shift, qkvg)


def spread_kernel(nr, nq, sides, pair, spread, strip, own_sem, send, recv, row_send, row_recv):
    r, q = lax.axis_index("row"), lax.axis_index("col")
    devices = nr * nq
    me = q * nr + r
    others = [lax.rem(me + d, devices) for d in range(1, devices)]
    places = [(lax.rem(other, nr), other // nr) for other in others]
    greet(places)
    copies = []
    for d in range(devices - 1):
        copies.append(
            pltpu.make_async_remote_copy(
                src_ref=sides.at[others[d]],
                dst_ref=spread.at[me],
                send_sem=send.at[d],
                recv_sem=recv.at[d],
                device_id=places[d],
                device_id_type=MESH,
            )
        )
        copies[-1].start()
    for e in range(1, nr):
        partner = lax.rem(r + e, nr)
        copies.append(
            pltpu.make_async_remote_copy(
                src_ref=pair.at[partner],
                dst_ref=strip.at[:, r],
                send_sem=row_send.at[e - 1],
                recv_sem=row_recv.at[e - 1],
                device_id=(partner, q),
                device_id_type=MESH,
            )
        )
        copies[-1].start()
    own = [
        pltpu.make_async_copy(sides.at[me], spread.at[me], own_sem.at[0]),
        pltpu.make_async_copy(pair.at[r], strip.at[:, r], own_sem.at[1]),
    ]
    for copy in own:
        copy.start()
    for copy in own:
        copy.wait()
    for copy in copies:
        copy.wait()


def spread_all(sides, pair, nr, nq):
    shape = (pair.shape[1], pair.shape[0]) + pair.shape[2:]
    return pl.pallas_call(
        functools.partial(spread_kernel, nr, nq),
        out_shape=[
            jax.ShapeDtypeStruct(sides.shape, sides.dtype),
            jax.ShapeDtypeStruct(shape, pair.dtype),
        ],
        in_specs=[pl.BlockSpec(memory_space=pltpu.VMEM)] * 2,
        out_specs=[pl.BlockSpec(memory_space=pltpu.VMEM)] * 2,
        scratch_shapes=[
            pltpu.SemaphoreType.DMA((2,)),
            pltpu.SemaphoreType.DMA((nr * nq - 1,)),
            pltpu.SemaphoreType.DMA((nr * nq - 1,)),
            pltpu.SemaphoreType.DMA((nr - 1,)),
            pltpu.SemaphoreType.DMA((nr - 1,)),
        ],
        compiler_params=pltpu.CompilerParams(
            collective_id=1, has_side_effects=True, vmem_limit_bytes=VMEM_LIMIT
        ),
    )(sides, pair)


def cut_spec(shape, dim, steps):
    block = tuple(n // steps if d == dim else n for d, n in enumerate(shape))
    return pl.BlockSpec(block, lambda c: tuple(c if d == dim else 0 for d in range(len(shape))))


def step_call(kernel, steps, ins, outs):
    return pl.pallas_call(
        kernel,
        grid=(steps,),
        in_specs=[cut_spec(a.shape, dim, steps) for a, dim in ins],
        out_specs=[cut_spec(shape, dim, steps) for shape, _, dim in outs],
        out_shape=[jax.ShapeDtypeStruct(shape, t) for shape, t, _ in outs],
        compiler_params=pltpu.CompilerParams(vmem_limit_bytes=VMEM_LIMIT),
    )(*[a for a, _ in ins])


def attend_and_return(ins, nr):
    columns, residues, channels = ins[0][0].shape
    block = (residues // nr, channels)
    return pl.pallas_call(
        functools.partial(attention_kernel, nr, columns),
        grid=(columns,),
        in_specs=[cut_spec(a.shape, dim, columns) for a, dim in ins],
        out_specs=pl.BlockSpec(memory_space=pl.ANY),
        out_shape=jax.ShapeDtypeStruct((nr, columns) + block, BF16),
        scratch_shapes=[
            pltpu.VMEM((columns, nr) + block, BF16),
            pltpu.SemaphoreType.DMA((columns,)),
            pltpu.SemaphoreType.DMA((nr - 1, columns)),
            pltpu.SemaphoreType.DMA((nr - 1, columns)),
        ],
        compiler_params=pltpu.CompilerParams(
            collective_id=2, has_side_effects=True, vmem_limit_bytes=VMEM_LIMIT
        ),
    )(*[a for a, _ in ins])


def on_device(
    pair,
    block_chain,
    block_valid,
    tri_norm_gain,
    tri_norm_bias,
    tri_in_weight,
    tri_gate_weight,
    out_norm_gain,
    out_norm_bias,
    tri_out_weight,
    att_norm_gain,
    att_norm_bias,
    qkvg_weight,
    bias_weight,
    inter_chain,
    att_out_weight,
):
    row_count, col_count, channels = pair.shape
    hidden = tri_out_weight.shape[0]
    row_devices = lax.axis_size("row")
    col_devices = lax.axis_size("col")
    devices = row_devices * col_devices
    residues = row_count * row_devices
    strip = col_count // row_devices
    axes = ("col", "row")
    residue_valid = jnp.repeat(block_valid, MB).astype(F32)
    residue_chain = jnp.repeat(block_chain, MB)
    strip_start = lax.axis_index("col") * col_count + lax.axis_index("row") * strip
    valid_j = lax.dynamic_slice_in_dim(residue_valid, strip_start, strip)[:, None]

    share = hidden // devices
    flat = strip * residues
    steps = strip // 2 if strip % 2 == 0 else 1
    by_column = jnp.swapaxes(pair, 0, 1)
    in_t = (
        tri_in_weight.reshape(channels, 2, 2, devices, share)
        .transpose(2, 3, 1, 4, 0)
        .reshape(4 * hidden, channels)
    )
    valid_rows = lax.dynamic_slice_in_dim(
        residue_valid, lax.axis_index("row") * row_count, row_count
    )
    valid_cols = lax.dynamic_slice_in_dim(
        residue_valid, lax.axis_index("col") * col_count, col_count
    )
    mask = (valid_cols[:, None] * valid_rows[None, :]).reshape(1, flat)
    (sides,) = step_call(
        project_kernel,
        steps,
        [
            (by_column, 0),
            (mask, 1),
            (tri_norm_gain[None, :], None),
            (tri_norm_bias[None, :], None),
            (in_t, None),
        ],
        [((2 * hidden, flat), BF16, 1)],
    )
    spread, own = spread_all(
        sides.reshape(devices, 2 * share, flat),
        by_column.reshape(row_devices, strip, row_count, channels),
        row_devices,
        col_devices,
    )
    own = own.reshape(strip, residues, channels)
    (tri_gate,) = step_call(
        gate_kernel,
        steps,
        [
            (own, 0),
            (tri_norm_gain[None, :], None),
            (tri_norm_bias[None, :], None),
            (tri_gate_weight, None),
        ],
        [((strip, residues, channels), F32, 0)],
    )
    product = pl.pallas_call(
        product_kernel,
        grid=(col_devices,),
        in_specs=[cut_spec(spread.shape, 0, col_devices)],
        out_specs=cut_spec((share, residues, residues), None, col_devices),
        out_shape=jax.ShapeDtypeStruct((share, residues, residues), BF16),
        scratch_shapes=[pltpu.VMEM((2 * share, residues, residues), F32)],
        compiler_params=pltpu.CompilerParams(vmem_limit_bytes=VMEM_LIMIT),
    )(spread)
    product = jnp.swapaxes(product.reshape(share, devices, flat), 0, 1)
    product = lax.all_to_all(product, axes, split_axis=0, concat_axis=0, tiled=True)
    mid, bias = step_call(
        middle_kernel,
        steps,
        [
            (own, 0),
            (product.reshape(hidden, flat), 1),
            (tri_gate, 0),
            (out_norm_gain[:, None], None),
            (out_norm_bias[:, None], None),
            (tri_out_weight, None),
            (att_norm_gain[None, :], None),
            (att_norm_bias[None, :], None),
            (bias_weight.T, None),
        ],
        [((strip, residues, channels), BF16, 0), ((strip, H, residues), BF16, 0)],
    )
    bias, qkv, gate = gather_all(
        bias,
        mid,
        att_norm_gain[None, :],
        att_norm_bias[None, :],
        qkvg_weight,
        row_devices,
        col_devices,
    )
    bias = bias.reshape(residues, H, residues)
    crossing = (residue_chain[:, None] != residue_chain[None, :]).astype(F32)
    extra = (
        jnp.swapaxes(bias, 0, 1).astype(F32)
        + inter_chain[:, None, None] * crossing[None]
        + (MASK_NEG * (residue_valid - 1.0))[None, None, :]
    )
    extra = jnp.pad(extra, ((0, 0), (0, 0), (0, -residues % 128)), constant_values=FILLED)
    result = attend_and_return(
        [
            (mid, 0),
            (extra, None),
            (residue_valid[:, None], None),
            (valid_j[:, :, None], 0),
            (qkv, 0),
            (gate, 0),
            (att_out_weight, None),
        ],
        row_devices,
    ).reshape(col_count, row_count, channels)
    return jnp.swapaxes(result, 0, 1)


def solution(mesh):
    placed = (P("row", "col", None),) + (P(),) * 15
    return jax.shard_map(
        on_device, mesh=mesh, in_specs=placed, out_specs=P("row", "col", None), check_vma=False
    )
```
